256 devices in a mesh: seg: 4 (over y_hi, core), fsdp: 64 (over x, z, y_lo).
Axes of the slice: x: 4, y: 4 (y_hi: 2, y_lo: 2; y = y_hi * 2 + y_lo), z: 8, core: 2. Of those that a mesh axis runs over, the one named last changes fastest.
Arguments:
- hidden: bfloat16 [64, 512, 8192], P('fsdp', 'seg'), may hold values from -6 to 6
- value_states: bfloat16 [64, 512, 8192], P('fsdp', 'seg'), may hold values from -6 to 6
- w_in: bfloat16 [8192, 128], P('fsdp'), may hold values from -0.0625 to 0.0625
- w_beta: bfloat16 [8192], P('fsdp'), may hold values from -0.0625 to 0.0625
- book_ids: int32 [64, 4], P('fsdp'), may hold values from 0 to 3, as said below
Outputs:
- mixed: bfloat16 [64, 512, 8192], P('fsdp', 'seg')
The draws below stay inside these ranges and needn't reach their ends.
Inputs may be any that keep to these rules, and one draw needn't show every extreme that they name: `book_ids`: each row starts at 0 and never falls along the segments, rising by at most one from one segment to the next; a rise marks the first segment of a new book.
All inputs are finite; a program needn't handle non-finite values.
Results may differ from the reference program's by a relative error of at most 0.0075.
Values may be sent and summed in bfloat16 or wider, within the bound.
A program may use at most 128 MiB of HBM per device.

```python
import jax
import jax.numpy as jnp
from jax import lax

D = 8192
SEG = 128
DK = 64
NU = 3
PHI = 384
LEN = 512
BOOKS = 64
N_SEG = 4


def draw_book_ids(key, part):
    key = jax.random.fold_in(key, 7)
    rolled = jax.random.randint(key, (BOOKS, N_SEG), 0, 4)
    starts = (rolled == 0).astype(jnp.int32)
    starts = starts.at[0, :].set(1)
    starts = starts.at[:, 0].set(0)
    return jnp.cumsum(starts, axis=1).astype(jnp.int32)


def shard_levels(stream_key, shape, cuts, low, largest):
    def one(dim, parts):
        heights = jax.random.uniform(jax.random.fold_in(jax.random.fold_in(stream_key, 6), dim), (parts,), jnp.float32, low / len(cuts), largest / len(cuts))
        return jnp.repeat(jnp.exp(heights), shape[dim] // parts).reshape((-1,) + (1,) * (len(shape) - dim - 1))

    factor_of = one(*cuts[0])
    for cut in cuts[1:]:
        factor_of = factor_of * one(*cut)
    return factor_of


def noise(stream_key, dims, scale, bound, shards=(), dtype=jnp.bfloat16):
    array = scale * jax.random.normal(stream_key, dims, jnp.float32)
    if shards:
        array = array * shard_levels(stream_key, dims, shards, -0.22, 0.18)
    return jnp.clip(array, -bound, bound).astype(dtype)


def setup_inputs(seed: int = 0) -> dict:
    streams_of = jax.random.split(jax.random.key(seed), 6)
    return {
        "hidden": noise(streams_of[0], (BOOKS, LEN, D), 1.0, 6.0, ((0, 64), (1, 4))),
        "value_states": noise(streams_of[1], (BOOKS, LEN, D), 1.0, 6.0, ((0, 64), (1, 4))),
        "w_in": noise(streams_of[2], (D, 2 * DK), D ** -0.5, 0.0625, ((0, 64),)),
        "w_beta": noise(streams_of[3], (D,), D ** -0.5, 0.0625, ((0, 64),)),
        "book_ids": draw_book_ids(jax.random.fold_in(streams_of[5], 71), 0),
    }


def feature_map(values_in):
    doubled = jnp.concatenate([jax.nn.relu(values_in), jax.nn.relu(-values_in)], axis=-1)
    return jnp.concatenate([doubled * jnp.roll(doubled, shift_by, axis=-1) for shift_by in range(1, NU + 1)], axis=-1)


def reference(hidden, value_states, w_in, w_beta, book_ids):
    highest = lax.Precision.HIGHEST

    def one_book(packed):
        tokens, value_rows, book_row = packed
        projected = jnp.dot(tokens, w_in, preferred_element_type=jnp.float32)
        beta_gate = jax.nn.sigmoid(jnp.dot(tokens, w_beta, preferred_element_type=jnp.float32))
        phi_q = feature_map(projected[:, :DK])
        phi_k = feature_map(projected[:, DK:2 * DK])
        values_all = value_rows.astype(jnp.float32)
        memory = jnp.zeros((PHI, D), jnp.bfloat16)
        normer = jnp.zeros((PHI,), jnp.float32)
        outputs = []
        for segment in range(N_SEG):
            lower = segment * SEG
            if segment > 0:
                continues = (book_row[segment] == book_row[segment - 1]).astype(jnp.float32)
            else:
                continues = jnp.zeros((), jnp.float32)
            mem_in = continues * memory.astype(jnp.float32)
            norm_in = continues * normer
            query_feat = phi_q[lower:lower + SEG]
            key_feat = phi_k[lower:lower + SEG]
            gate_seg = beta_gate[lower:lower + SEG]
            value_seg = values_all[lower:lower + SEG]
            query_div = jnp.maximum(jnp.dot(query_feat, norm_in, precision=highest), 1.0)
            outputs.append((jnp.dot(query_feat, mem_in, precision=highest) / query_div[:, None]).astype(jnp.bfloat16))
            key_div = jnp.maximum(jnp.dot(key_feat, norm_in, precision=highest), 1.0)
            recalled = jnp.dot(key_feat, mem_in, precision=highest)
            update = gate_seg[:, None] * value_seg - (gate_seg / key_div)[:, None] * recalled
            memory = (mem_in + jnp.dot(key_feat.T, update, precision=highest)).astype(jnp.bfloat16)
            normer = norm_in + jnp.sum(key_feat, axis=0)
        return jnp.concatenate(outputs, axis=0)

    return lax.map(one_book, (hidden, value_states, book_ids))
```

```python
import functools

import jax
import jax.numpy as jnp
from jax import lax
from jax.experimental import pallas as pl
from jax.experimental.pallas import tpu as pltpu
from jax.sharding import PartitionSpec as P

NU = 3
X, Z, YL, SEGS = 4, 8, 2, 4
CHUNK = 512
EARLY = 12
MESH = pl.DeviceIdType.MESH
HIGHEST = lax.Precision.HIGHEST
F32, BF16 = jnp.float32, jnp.bfloat16


def dot(a, b):
    return jnp.dot(a, b, precision=HIGHEST, preferred_element_type=F32)


def dot_t(a, b):
    return lax.dot_general(
        a, b, (((1,), (1,)), ((), ())), precision=HIGHEST, preferred_element_type=F32
    )


def halves(u, turned, low):
    return jnp.where(low, jnp.maximum(u, 0.0), jnp.maximum(-turned, 0.0))


def phi_of(p):
    return jnp.concatenate([p * pltpu.roll(p, j, 1) for j in range(1, NU + 1)], axis=1)


def kernel(
    hidden, values, w_in, w_beta, ids, out,
    hid, wbuf, vbuf, kown, kbuf, m_hi, m_lo, acc, lacc,
    hid_sem, y_send, y_recv, x_send, x_recv, zr_send, zr_recv, zl_send, zl_recv,
    s_send, s_recv, k_send, k_recv, v_send, v_recv, r_send, r_recv, d_send, d_recv,
):
    s, f = lax.axis_index("seg"), lax.axis_index("fsdp")
    core, yl = lax.rem(s, 2), lax.rem(f, YL)
    z = lax.rem(lax.div(f, YL), Z)
    x = lax.div(f, YL * Z)
    tokens, width = hid.shape
    chunks = width // CHUNK

    def at(x_, z_, yl_):
        return (x_ * Z + z_) * YL + yl_

    sib = (s + 1 - 2 * core, f)
    cross = (lax.rem(s + 2, SEGS), f)
    y_peer = (s, at(x, z, 1 - yl))
    x_peer = [(s, at(lax.rem(x + d, X), z, yl)) for d in range(1, X)]
    right = (s, at(x, lax.rem(z + 1, Z), yl))
    left = (s, at(x, lax.rem(z + Z - 1, Z), yl))

    def remote(src, dst, send, recv, to):
        return pltpu.make_async_remote_copy(
            src_ref=src, dst_ref=dst, send_sem=send, recv_sem=recv, device_id=to, device_id_type=MESH
        )

    barrier = pltpu.get_barrier_semaphore()
    peers = [cross, sib, y_peer, *x_peer, right, left]
    for peer in peers:
        pl.semaphore_signal(barrier, inc=1, device_id=peer, device_id_type=MESH)
    hid_copy = pltpu.make_async_copy(hidden, hid, hid_sem)
    hid_copy.start()
    for r in range(SEGS - 1):

        @pl.when(s <= r)
        def _(r=r):
            kbuf[r] = jnp.zeros(kbuf.shape[1:], F32)

    own = wbuf.at[core, z, x]
    owner = core == yl

    @pl.when(owner)
    def _():
        wbuf[core, z, x, 0:128, :] = w_in[...]
        wbuf[core, z, x, 128:144, :] = jnp.broadcast_to(w_beta[...], (16, 128))

    pl.semaphore_wait(barrier, len(peers))

    y_copy = remote(own, own, y_send, y_recv, y_peer)
    pl.when(owner)(y_copy.start)

    def columns(k):
        return pl.ds(pl.multiple_of(k * CHUNK, CHUNK), CHUNK)

    def v_copy(k, slot):
        c = columns(k)
        return remote(values.at[:, c], vbuf.at[slot, :, c], v_send.at[k], v_recv.at[k], cross)

    def v_start(lo, hi):
        @pl.when(s < 2)
        def _():
            pl.loop(lo, hi)(lambda k: v_copy(k, s).start())

    v_start(0, EARLY)

    pl.when(jnp.logical_not(owner))(y_copy.wait_recv)
    x_copies = [
        remote(own, own, x_send.at[i], x_recv.at[i], peer) for i, peer in enumerate(x_peer)
    ]
    for c in x_copies:
        c.start()
    hid_copy.wait()
    acc[...] = jnp.zeros_like(acc)
    lacc[...] = jnp.zeros_like(lacc)
    for c in x_copies:
        c.wait_recv()

    def block(d):
        return lax.rem(z + d + Z, Z)

    def to_sib(i, d):
        b = wbuf.at[core, block(d)]
        return remote(b, b, s_send.at[i], s_recv.at[i], sib)

    def project(d):
        zb = block(d)

        @pl.loop(0, YL * X)
        def _(q):
            p, xb = lax.div(q, X), lax.rem(q, X)
            lo = pl.multiple_of(at(xb, zb, p) * 128, 128)
            h = hid[:, pl.ds(lo, 128)]
            acc[...] += jnp.dot(h, wbuf[p, zb, xb, 0:128, :], preferred_element_type=F32)
            lacc[...] += h.astype(F32) * wbuf[p, zb, xb, 128:144, :][0:1].astype(F32)

    half = Z // 2

    def ring(t):
        lo, n = (0, X) if t < half else (0, X // 2)
        a = wbuf.at[core, block(1 - t), pl.ds(lo, n)]
        to_r = remote(a, a, zr_send.at[t - 1], zr_recv.at[t - 1], right)
        lo = 0 if t < half else X // 2
        b = wbuf.at[core, block(t - 1), pl.ds(lo, n)]
        to_l = remote(b, b, zl_send.at[t - 1], zl_recv.at[t - 1], left)
        return to_r, to_l

    ring_copies = []
    order = [0]
    sib_copies = [to_sib(0, 0)]
    for t in range(1, half + 1):
        step = ring(t)
        for c in step:
            c.start()
        ring_copies.extend(step)
        fresh = sib_copies[-1:] if t == 1 else sib_copies[-2:]
        for c in fresh:
            c.start()
        if t > 1:
            for i in ([0] if t == 2 else [2 * t - 5, 2 * t - 4]):
                sib_copies[i].wait_recv()
                project(order[i])
        for c in step:
            c.wait_recv()
        if t < half:
            order += [-t, t]
            sib_copies += [to_sib(2 * t - 1, -t), to_sib(2 * t, t)]
        else:
            order += [half]
            sib_copies += [to_sib(2 * t - 1, half)]
    sib_copies[-1].start()
    for i in range(2 * half - 3, 2 * half):
        sib_copies[i].wait_recv()
        project(order[i])

    low = lax.broadcasted_iota(jnp.int32, (tokens, 128), 1) < 64
    low_half = low[: tokens // 2]
    proj = acc[...]
    turned = pltpu.roll(proj, 64, 1)
    logit = dot_t(jnp.ones((8, 128), F32), lacc[...])
    kown[0:64, :] = jnp.where(low_half, turned[0:64], proj[64:128])
    kown[64:72, :] = 1.0 / (1.0 + jnp.exp(-logit))

    def k_copy(src, r, i, to):
        return remote(src, kbuf.at[r], k_send.at[i], k_recv.at[r], to)

    @pl.when(s < 2)
    def _():
        k_copy(kown, s, 0, cross).start()

    v_start(EARLY, chunks)

    @pl.when(core == 0)
    def _():
        k_copy(kown, s, 1, sib).start()

    v_sib = remote(values, vbuf.at[s], d_send, d_recv, sib)
    pl.when(core == 0)(v_sib.start)

    phi_q = phi_of(halves(proj, turned, low))

    held = lax.rem(s, 2)

    @pl.when(s >= 2)
    def _():
        k_copy(kown, held, 0, cross).wait_recv()
        k_copy(kbuf.at[held], held, 2, sib).start()
        k_copy(kown, 1 - held, 0, sib).wait_recv()

    @pl.when(s == 1)
    def _():
        k_copy(kown, 0, 0, sib).wait_recv()

    @pl.when(s == 3)
    def _():
        k_copy(kown, 2, 0, sib).wait_recv()

    @pl.when(s > 0)
    def _():
        keeps, phis, betas, gains = [], [], [], []
        norm = jnp.zeros((1, 128 * NU), F32)
        for r in range(SEGS - 1):
            two = kbuf[r, 0:64, :]
            two_turned = pltpu.roll(two, 64, 1)
            p = jnp.concatenate(
                [halves(two, two_turned, low_half), halves(two_turned, two, low_half)], axis=0
            )
            phi = phi_of(p)
            beta = kbuf[r, 64:72, :]
            div = jnp.maximum(dot_t(jnp.broadcast_to(norm, (8, 128 * NU)), phi), 1.0)
            keep = jnp.where((ids[0, r + 1] == ids[0, r]) | (s < r + 1), 1.0, 0.0).astype(F32)
            phis.append(phi)
            betas.append(beta[0:1])
            gains.append((beta / div)[0:1])
            keeps.append(keep)
            norm = keep * (norm + jnp.sum(phi, axis=0, keepdims=True))
        scale = 1.0 / jnp.maximum(jnp.sum(phi_q * norm, axis=1, keepdims=True), 1.0)
        q = phi_q
        for r in reversed(range(SEGS - 1)):
            q = keeps[r] * q
            t = dot_t(q, phis[r])
            m = t * betas[r] * scale
            hi = m.astype(BF16)
            m_hi[:, 128 * r : 128 * (r + 1)] = hi
            m_lo[:, 128 * r : 128 * (r + 1)] = (m - hi.astype(F32)).astype(BF16)
            if r:
                q = q - dot(t * gains[r], phis[r])

    def mix(k, n):
        c = columns(k)
        v = vbuf[0:n, :, c].reshape(128 * n, CHUNK)
        mixed = jnp.dot(m_hi[:, : 128 * n], v, preferred_element_type=F32)
        mixed += jnp.dot(m_lo[:, : 128 * n], v, preferred_element_type=F32)
        out[:, c] = mixed.astype(BF16)

    @pl.when(s == 0)
    def _():
        out[...] = jnp.zeros_like(out)

    @pl.when(s == 1)
    def _():
        remote(values, vbuf.at[0], d_send, d_recv, sib).wait_recv()
        pl.loop(0, chunks)(lambda k: mix(k, 1))

    def relay(k, slot):
        c = columns(k)
        b = vbuf.at[slot, :, c]
        return remote(b, b, r_send.at[k], r_recv.at[k], sib)

    @pl.when(s >= 2)
    def _():
        @pl.when(s == 3)
        def _():
            remote(values, vbuf.at[2], d_send, d_recv, sib).wait_recv()

        def take(k):
            v_copy(k, held).wait_recv()
            relay(k, held).start()

        def use(k):
            relay(k, 1 - held).wait_recv()
            pl.when(s == 2)(lambda: mix(k, 2))
            pl.when(s == 3)(lambda: mix(k, 3))

        take(0)

        @pl.loop(1, chunks)
        def _(k):
            take(k)
            use(k - 1)

        use(chunks - 1)
        pl.loop(0, chunks)(lambda k: relay(k, held).wait_send())
        k_copy(kbuf.at[held], held, 2, sib).wait_send()

    pl.when(owner)(y_copy.wait_send)
    for c in (*x_copies, *ring_copies, *sib_copies):
        c.wait_send()

    @pl.when(s < 2)
    def _():
        pl.loop(0, chunks)(lambda k: v_copy(k, s).wait_send())
        k_copy(kown, s, 0, cross).wait_send()

    @pl.when(core == 0)
    def _():
        k_copy(kown, s, 1, sib).wait_send()
        v_sib.wait_send()


def per_device(hidden, value_states, w_in, w_beta, book_ids):
    _, tokens, width = hidden.shape
    chunks = width // CHUNK
    dma = pltpu.SemaphoreType.DMA
    vmem = pl.BlockSpec(memory_space=pltpu.VMEM)
    hbm = pl.BlockSpec(memory_space=pl.ANY)
    mixed = pl.pallas_call(
        kernel,
        out_shape=jax.ShapeDtypeStruct((tokens, width), BF16),
        in_specs=[hbm, hbm, vmem, vmem, pl.BlockSpec(memory_space=pltpu.SMEM)],
        out_specs=vmem,
        scratch_shapes=[
            pltpu.VMEM((tokens, width), BF16),
            pltpu.VMEM((YL, Z, X, 144, 128), BF16),
            pltpu.VMEM((SEGS - 1, tokens, width), BF16),
            pltpu.VMEM((72, 128), F32),
            pltpu.VMEM((SEGS - 1, 72, 128), F32),
            pltpu.VMEM((tokens, 128 * (SEGS - 1)), BF16),
            pltpu.VMEM((tokens, 128 * (SEGS - 1)), BF16),
            pltpu.VMEM((tokens, 128), F32),
            pltpu.VMEM((tokens, 128), F32),
            dma, dma, dma, dma((X - 1,)), dma((X - 1,)),
            dma((Z // 2,)), dma((Z // 2,)), dma((Z // 2,)), dma((Z // 2,)),
            dma((Z,)), dma((Z,)), dma((3,)), dma((SEGS - 1,)),
            dma((chunks,)), dma((chunks,)), dma((chunks,)), dma((chunks,)), dma, dma,
        ],
        compiler_params=pltpu.CompilerParams(
            collective_id=0, has_side_effects=True, vmem_limit_bytes=32 << 20
        ),
    )(hidden[0], value_states[0], w_in, w_beta.reshape(1, 128), book_ids)
    return mixed[None]


def solution(mesh):
    return jax.shard_map(
        per_device,
        mesh=mesh,
        in_specs=(
            P("fsdp", "seg", None),
            P("fsdp", "seg", None),
            P("fsdp", None),
            P("fsdp"),
            P("fsdp", None),
        ),
        out_specs=P("fsdp", "seg", None),
        check_vma=False,
    )
```

```python
import functools

import jax
import jax.numpy as jnp
from jax import lax
from jax.experimental import pallas as pl
from jax.experimental.pallas import tpu as pltpu
from jax.sharding import PartitionSpec as P

NU = 3
X, Z, YL, SEGS = 4, 8, 2, 4
CHUNK = 512
EARLY = 12
MESH = pl.DeviceIdType.MESH
HIGHEST = lax.Precision.HIGHEST
F32, BF16 = jnp.float32, jnp.bfloat16


def dot(a, b):
    return jnp.dot(a, b, precision=HIGHEST, preferred_element_type=F32)


def dot_t(a, b):
    return lax.dot_general(
        a, b, (((1,), (1,)), ((), ())), precision=HIGHEST, preferred_element_type=F32
    )


def halves(u, turned, low):
    return jnp.where(low, jnp.maximum(u, 0.0), jnp.maximum(-turned, 0.0))


def phi_of(p):
    return jnp.concatenate([p * pltpu.roll(p, j, 1) for j in range(1, NU + 1)], axis=1)


def kernel(
    hidden, values, w_in, w_beta, ids, out,
    hid, wbuf, vbuf, kown, kbuf, m_hi, m_lo, acc, lacc,
    wb, idm, hid_sem, w_sem, wb_sem, id_sem, y_send, y_recv, x_send, x_recv, zr_send, zr_recv, zl_send, zl_recv,
    s_send, s_recv, k_send, k_recv, v_send, v_recv, r_send, r_recv, d_send, d_recv,
):
    s, f = lax.axis_index("seg"), lax.axis_index("fsdp")
    core, yl = lax.rem(s, 2), lax.rem(f, YL)
    z = lax.rem(lax.div(f, YL), Z)
    x = lax.div(f, YL * Z)
    tokens, width = hid.shape
    chunks = width // CHUNK

    def at(x_, z_, yl_):
        return (x_ * Z + z_) * YL + yl_

    sib = (s + 1 - 2 * core, f)
    cross = (lax.rem(s + 2, SEGS), f)
    y_peer = (s, at(x, z, 1 - yl))
    x_peer = [(s, at(lax.rem(x + d, X), z, yl)) for d in range(1, X)]
    right = (s, at(x, lax.rem(z + 1, Z), yl))
    left = (s, at(x, lax.rem(z + Z - 1, Z), yl))

    def remote(src, dst, send, recv, to):
        return pltpu.make_async_remote_copy(
            src_ref=src, dst_ref=dst, send_sem=send, recv_sem=recv, device_id=to, device_id_type=MESH
        )

    barrier = pltpu.get_barrier_semaphore()
    peers = [cross, sib, y_peer, *x_peer, right, left]
    for peer in peers:
        pl.semaphore_signal(barrier, inc=1, device_id=peer, device_id_type=MESH)
    hid_copy = pltpu.make_async_copy(hidden, hid, hid_sem)
    own = wbuf.at[core, z, x]
    owner = core == yl
    w_copy = pltpu.make_async_copy(w_in, wbuf.at[core, z, x, pl.ds(0, 128)], w_sem)
    wb_copy = pltpu.make_async_copy(w_beta, wb, wb_sem)
    id_copy = pltpu.make_async_copy(ids, idm, id_sem)

    @pl.when(owner)
    def _():
        w_copy.start()
        wb_copy.start()

    hid_copy.start()
    id_copy.start()
    for r in range(SEGS - 1):

        @pl.when(s <= r)
        def _(r=r):
            kbuf[r] = jnp.zeros(kbuf.shape[1:], F32)

    @pl.when(owner)
    def _():
        wb_copy.wait()
        wbuf[core, z, x, 128:144, :] = jnp.broadcast_to(wb[...], (16, 128))
        w_copy.wait()

    pl.semaphore_wait(barrier, len(peers))

    y_copy = remote(own, own, y_send, y_recv, y_peer)
    pl.when(owner)(y_copy.start)

    def columns(k):
        return pl.ds(pl.multiple_of(k * CHUNK, CHUNK), CHUNK)

    def v_copy(k, slot):
        c = columns(k)
        return remote(values.at[:, c], vbuf.at[slot, :, c], v_send.at[k], v_recv.at[k], cross)

    def v_start(lo, hi):
        @pl.when(s < 2)
        def _():
            pl.loop(lo, hi)(lambda k: v_copy(k, s).start())

    v_start(0, EARLY)

    pl.when(jnp.logical_not(owner))(y_copy.wait_recv)
    x_copies = [
        remote(own, own, x_send.at[i], x_recv.at[i], peer) for i, peer in enumerate(x_peer)
    ]
    for c in x_copies:
        c.start()
    hid_copy.wait()
    id_copy.wait()
    acc[...] = jnp.zeros_like(acc)
    lacc[...] = jnp.zeros_like(lacc)
    for c in x_copies:
        c.wait_recv()

    def block(d):
        return lax.rem(z + d + Z, Z)

    def to_sib(i, d):
        b = wbuf.at[core, block(d)]
        return remote(b, b, s_send.at[i], s_recv.at[i], sib)

    def project(d):
        zb = block(d)

        @pl.loop(0, YL * X)
        def _(q):
            p, xb = lax.div(q, X), lax.rem(q, X)
            lo = pl.multiple_of(at(xb, zb, p) * 128, 128)
            h = hid[:, pl.ds(lo, 128)]
            acc[...] += jnp.dot(h, wbuf[p, zb, xb, 0:128, :], preferred_element_type=F32)
            lacc[...] += h.astype(F32) * wbuf[p, zb, xb, 128:144, :][0:1].astype(F32)

    half = Z // 2

    def ring(t):
        lo, n = (0, X) if t < half else (0, X // 2)
        a = wbuf.at[core, block(1 - t), pl.ds(lo, n)]
        to_r = remote(a, a, zr_send.at[t - 1], zr_recv.at[t - 1], right)
        lo = 0 if t < half else X // 2
        b = wbuf.at[core, block(t - 1), pl.ds(lo, n)]
        to_l = remote(b, b, zl_send.at[t - 1], zl_recv.at[t - 1], left)
        return to_r, to_l

    ring_copies = []
    order = [0]
    sib_copies = [to_sib(0, 0)]
    for t in range(1, half + 1):
        step = ring(t)
        for c in step:
            c.start()
        ring_copies.extend(step)
        fresh = sib_copies[-1:] if t == 1 else sib_copies[-2:]
        for c in fresh:
            c.start()
        if t > 1:
            for i in ([0] if t == 2 else [2 * t - 5, 2 * t - 4]):
                sib_copies[i].wait_recv()
                project(order[i])
        for c in step:
            c.wait_recv()
        if t < half:
            order += [-t, t]
            sib_copies += [to_sib(2 * t - 1, -t), to_sib(2 * t, t)]
        else:
            order += [half]
            sib_copies += [to_sib(2 * t - 1, half)]
    sib_copies[-1].start()
    for i in range(2 * half - 3, 2 * half):
        sib_copies[i].wait_recv()
        project(order[i])

    low = lax.broadcasted_iota(jnp.int32, (tokens, 128), 1) < 64
    low_half = low[: tokens // 2]
    proj = acc[...]
    turned = pltpu.roll(proj, 64, 1)
    logit = dot_t(jnp.ones((8, 128), F32), lacc[...])
    kown[0:64, :] = jnp.where(low_half, turned[0:64], proj[64:128])
    kown[64:72, :] = 1.0 / (1.0 + jnp.exp(-logit))

    def k_copy(src, r, i, to):
        return remote(src, kbuf.at[r], k_send.at[i], k_recv.at[r], to)

    @pl.when(s < 2)
    def _():
        k_copy(kown, s, 0, cross).start()

    v_start(EARLY, chunks)

    @pl.when(core == 0)
    def _():
        k_copy(kown, s, 1, sib).start()

    v_sib = remote(values, vbuf.at[s], d_send, d_recv, sib)
    pl.when(core == 0)(v_sib.start)

    phi_q = phi_of(halves(proj, turned, low))

    held = lax.rem(s, 2)

    @pl.when(s >= 2)
    def _():
        k_copy(kown, held, 0, cross).wait_recv()
        k_copy(kbuf.at[held], held, 2, sib).start()
        k_copy(kown, 1 - held, 0, sib).wait_recv()

    @pl.when(s == 1)
    def _():
        k_copy(kown, 0, 0, sib).wait_recv()

    @pl.when(s == 3)
    def _():
        k_copy(kown, 2, 0, sib).wait_recv()

    @pl.when(s > 0)
    def _():
        keeps, phis, betas, gains = [], [], [], []
        norm = jnp.zeros((1, 128 * NU), F32)
        for r in range(SEGS - 1):
            two = kbuf[r, 0:64, :]
            two_turned = pltpu.roll(two, 64, 1)
            p = jnp.concatenate(
                [halves(two, two_turned, low_half), halves(two_turned, two, low_half)], axis=0
            )
            phi = phi_of(p)
            beta = kbuf[r, 64:72, :]
            div = jnp.maximum(dot_t(jnp.broadcast_to(norm, (8, 128 * NU)), phi), 1.0)
            keep = jnp.where((idm[0, r + 1] == idm[0, r]) | (s < r + 1), 1.0, 0.0).astype(F32)
            phis.append(phi)
            betas.append(beta[0:1])
            gains.append((beta / div)[0:1])
            keeps.append(keep)
            norm = keep * (norm + jnp.sum(phi, axis=0, keepdims=True))
        scale = 1.0 / jnp.maximum(jnp.sum(phi_q * norm, axis=1, keepdims=True), 1.0)
        q = phi_q
        for r in reversed(range(SEGS - 1)):
            q = keeps[r] * q
            t = dot_t(q, phis[r])
            m = t * betas[r] * scale
            hi = m.astype(BF16)
            m_hi[:, 128 * r : 128 * (r + 1)] = hi
            m_lo[:, 128 * r : 128 * (r + 1)] = (m - hi.astype(F32)).astype(BF16)
            if r:
                q = q - dot(t * gains[r], phis[r])

    def mix(k, n):
        c = columns(k)
        v = vbuf[0:n, :, c].reshape(128 * n, CHUNK)
        mixed = jnp.dot(m_hi[:, : 128 * n], v, preferred_element_type=F32)
        mixed += jnp.dot(m_lo[:, : 128 * n], v, preferred_element_type=F32)
        out[:, c] = mixed.astype(BF16)

    @pl.when(s == 0)
    def _():
        out[...] = jnp.zeros_like(out)

    @pl.when(s == 1)
    def _():
        remote(values, vbuf.at[0], d_send, d_recv, sib).wait_recv()
        pl.loop(0, chunks)(lambda k: mix(k, 1))

    def relay(k, slot):
        c = columns(k)
        b = vbuf.at[slot, :, c]
        return remote(b, b, r_send.at[k], r_recv.at[k], sib)

    @pl.when(s >= 2)
    def _():
        @pl.when(s == 3)
        def _():
            remote(values, vbuf.at[2], d_send, d_recv, sib).wait_recv()

        def take(k):
            v_copy(k, held).wait_recv()
            relay(k, held).start()

        def use(k):
            relay(k, 1 - held).wait_recv()
            pl.when(s == 2)(lambda: mix(k, 2))
            pl.when(s == 3)(lambda: mix(k, 3))

        take(0)

        @pl.loop(1, chunks)
        def _(k):
            take(k)
            use(k - 1)

        use(chunks - 1)
        pl.loop(0, chunks)(lambda k: relay(k, held).wait_send())
        k_copy(kbuf.at[held], held, 2, sib).wait_send()

    pl.when(owner)(y_copy.wait_send)
    for c in (*x_copies, *ring_copies, *sib_copies):
        c.wait_send()

    @pl.when(s < 2)
    def _():
        pl.loop(0, chunks)(lambda k: v_copy(k, s).wait_send())
        k_copy(kown, s, 0, cross).wait_send()

    @pl.when(core == 0)
    def _():
        k_copy(kown, s, 1, sib).wait_send()
        v_sib.wait_send()


def per_device(hidden, value_states, w_in, w_beta, book_ids):
    _, tokens, width = hidden.shape
    chunks = width // CHUNK
    dma = pltpu.SemaphoreType.DMA
    hbm = pl.BlockSpec(memory_space=pltpu.HBM)
    mixed = pl.pallas_call(
        kernel,
        out_shape=jax.ShapeDtypeStruct((tokens, width), BF16),
        in_specs=[hbm] * 5,
        out_specs=pl.BlockSpec(memory_space=pltpu.VMEM),
        scratch_shapes=[
            pltpu.VMEM((tokens, width), BF16),
            pltpu.VMEM((YL, Z, X, 144, 128), BF16),
            pltpu.VMEM((SEGS - 1, tokens, width), BF16),
            pltpu.VMEM((72, 128), F32),
            pltpu.VMEM((SEGS - 1, 72, 128), F32),
            pltpu.VMEM((tokens, 128 * (SEGS - 1)), BF16),
            pltpu.VMEM((tokens, 128 * (SEGS - 1)), BF16),
            pltpu.VMEM((tokens, 128), F32),
            pltpu.VMEM((tokens, 128), F32),
            pltpu.VMEM((1, 128), BF16), pltpu.SMEM((1, SEGS), jnp.int32),
            dma, dma, dma, dma, dma, dma, dma((X - 1,)), dma((X - 1,)),
            dma((Z // 2,)), dma((Z // 2,)), dma((Z // 2,)), dma((Z // 2,)),
            dma((Z,)), dma((Z,)), dma((3,)), dma((SEGS - 1,)),
            dma((chunks,)), dma((chunks,)), dma((chunks,)), dma((chunks,)), dma, dma,
        ],
        compiler_params=pltpu.CompilerParams(
            collective_id=0, has_side_effects=True, vmem_limit_bytes=32 << 20
        ),
    )(*(
        pltpu.with_memory_space_constraint(a, pltpu.HBM)
        for a in (hidden[0], value_states[0], w_in, w_beta.reshape(1, 128), book_ids)
    ))
    return mixed[None]


def solution(mesh):
    return jax.shard_map(
        per_device,
        mesh=mesh,
        in_specs=(
            P("fsdp", "seg", None),
            P("fsdp", "seg", None),
            P("fsdp", None),
            P("fsdp"),
            P("fsdp", None),
        ),
        out_specs=P("fsdp", "seg", None),
        check_vma=False,
    )
```

```python
import functools

import jax
import jax.numpy as jnp
from jax import lax
from jax.experimental import pallas as pl
from jax.experimental.pallas import tpu as pltpu
from jax.sharding import PartitionSpec as P

NU = 3
X, Z, YL, SEGS = 4, 8, 2, 4
X_ORDER = (1, 3, 2)
CHUNK = 512
EARLY = 5
HALFWAY = 8
MESH = pl.DeviceIdType.MESH
HIGHEST = lax.Precision.HIGHEST
F32, BF16 = jnp.float32, jnp.bfloat16


def dot(a, b):
    return jnp.dot(a, b, precision=HIGHEST, preferred_element_type=F32)


def dot_t(a, b):
    return lax.dot_general(
        a, b, (((1,), (1,)), ((), ())), precision=HIGHEST, preferred_element_type=F32
    )


def halves(u, turned, low):
    return jnp.where(low, jnp.maximum(u, 0.0), jnp.maximum(-turned, 0.0))


def phi_of(p):
    return jnp.concatenate([p * pltpu.roll(p, j, 1) for j in range(1, NU + 1)], axis=1)


def kernel(
    hidden, values, w_in, w_beta, ids, out,
    hid, wbuf, vbuf, kown, kbuf, m_hi, m_lo, acc, lacc,
    wb, idm, hid_sem, w_sem, wb_sem, id_sem, y_send, y_recv, x_send, x_recv, zr_send, zr_recv, zl_send, zl_recv,
    s_send, s_recv, k_send, k_recv, v_send, v_recv, r_send, r_recv, d_send, d_recv,
):
    s, f = lax.axis_index("seg"), lax.axis_index("fsdp")
    core, yl = lax.rem(s, 2), lax.rem(f, YL)
    z = lax.rem(lax.div(f, YL), Z)
    x = lax.div(f, YL * Z)
    tokens, width = hid.shape
    chunks = width // CHUNK
    first, second = core == 0, core == 1

    def at(x_, z_, yl_):
        return (x_ * Z + z_) * YL + yl_

    sib = (s + 1 - 2 * core, f)
    cross = (lax.rem(s + 2, SEGS), f)
    y_peer = (s, at(x, z, 1 - yl))
    x_peer = [(s, at(lax.rem(x + d, X), z, yl)) for d in X_ORDER]
    right = (s, at(x, lax.rem(z + 1, Z), yl))
    left = (s, at(x, lax.rem(z + Z - 1, Z), yl))

    def remote(src, dst, send, recv, to):
        return pltpu.make_async_remote_copy(
            src_ref=src, dst_ref=dst, send_sem=send, recv_sem=recv, device_id=to, device_id_type=MESH
        )

    barrier = pltpu.get_barrier_semaphore()
    near, far = [cross, sib], [y_peer, *x_peer, right, left]

    def greet(peers):
        for peer in peers:
            pl.semaphore_signal(barrier, inc=1, device_id=peer, device_id_type=MESH)

    greet(near)
    pl.when(second)(lambda: greet(far))
    hid_copy = pltpu.make_async_copy(hidden, hid, hid_sem)
    w_copy = pltpu.make_async_copy(w_in, wbuf.at[z, x, yl, pl.ds(0, 128)], w_sem)
    wb_copy = pltpu.make_async_copy(w_beta, wb, wb_sem)
    id_copy = pltpu.make_async_copy(ids, idm, id_sem)

    @pl.when(second)
    def _():
        w_copy.start()
        wb_copy.start()

    hid_copy.start()
    id_copy.start()
    for r in range(SEGS - 1):

        @pl.when(s <= r)
        def _(r=r):
            kbuf[r] = jnp.zeros(kbuf.shape[1:], F32)

    def columns(k):
        return pl.ds(pl.multiple_of(k * CHUNK, CHUNK), CHUNK)

    def v_copy(k, slot):
        c = columns(k)
        return remote(values.at[:, c], vbuf.at[slot, :, c], v_send.at[k], v_recv.at[k], cross)

    def v_start(lo, hi, slot):
        pl.loop(lo, hi)(lambda k: v_copy(k, slot).start())

    def project(zb):
        total = jnp.zeros((tokens, 128), F32)
        gate = jnp.zeros((tokens, 128), F32)
        for xb in range(X):
            lo = pl.multiple_of(at(xb, zb, 0) * 128, 128 * YL)
            h = hid[:, pl.ds(lo, 128 * YL)]
            w = jnp.concatenate([wbuf[zb, xb, p, 0:128, :] for p in range(YL)], axis=0)
            total += jnp.dot(h, w, preferred_element_type=F32)
            for p in range(YL):
                row = wbuf[zb, xb, p, 128:144, :][0:1].astype(F32)
                gate += h[:, 128 * p : 128 * (p + 1)].astype(F32) * row
        acc[...] += total
        lacc[...] += gate

    def block(d):
        return lax.rem(z + d + Z, Z)

    half = Z // 2
    order = [0] + [d for t in range(1, half) for d in (-t, t)] + [half]

    def to_sib(i):
        b = wbuf.at[block(order[i])]
        return remote(b, b, s_send.at[i], s_recv.at[i], sib)

    def clear():
        acc[...] = jnp.zeros_like(acc)
        lacc[...] = jnp.zeros_like(lacc)
        hid_copy.wait()
        id_copy.wait()

    own = wbuf.at[z, x, yl]
    y_copy = remote(own, own, y_send, y_recv, y_peer)
    pair = wbuf.at[z, x]
    x_copies = [
        remote(pair, pair, x_send.at[i], x_recv.at[i], peer) for i, peer in enumerate(x_peer)
    ]

    def ring(t, j):
        xs = lax.rem(x + X - (0, *X_ORDER)[j], X)
        copies = []
        if t < half or j < X // 2:
            b = wbuf.at[block(1 - t), xs]
            copies.append(remote(b, b, zr_send.at[t - 1, j], zr_recv.at[t - 1, j], right))
        if t < half or j >= X // 2:
            b = wbuf.at[block(t - 1), xs]
            copies.append(remote(b, b, zl_send.at[t - 1, j], zl_recv.at[t - 1, j], left))
        return copies

    rings = {(t, j): ring(t, j) for t in range(1, half + 1) for j in range(X)}

    @pl.when(first)
    def _():
        pl.semaphore_wait(barrier, len(near))
        pl.when(s == 0)(lambda: v_start(0, chunks, 0))
        clear()
        for i in range(Z):
            to_sib(i).wait_recv()
            project(block(order[i]))

    @pl.when(second)
    def _():
        wb_copy.wait()
        wbuf[z, x, yl, 128:144, :] = jnp.broadcast_to(wb[...], (16, 128))
        w_copy.wait()
        pl.semaphore_wait(barrier, len(near) + len(far))
        y_copy.start()
        pl.when(s == 1)(lambda: v_start(0, EARLY, 1))
        y_copy.wait_recv()
        for c in x_copies:
            c.start()
        for c in rings[1, 0]:
            c.start()
        clear()
        for j in range(1, X):
            x_copies[j - 1].wait_recv()
            for c in rings[1, j]:
                c.start()
        to_sib(0).start()
        project(block(0))
        for t in range(1, half + 1):
            for j in range(X):
                for c in rings[t, j]:
                    c.wait_recv()
                if t < half:
                    for c in rings[t + 1, j]:
                        c.start()
            for i in (2 * t - 1, 2 * t):
                if i < Z:
                    to_sib(i).start()
            for i in (2 * t - 1, 2 * t):
                if i < Z:
                    project(block(order[i]))

    low = lax.broadcasted_iota(jnp.int32, (tokens, 128), 1) < 64
    low_half = low[: tokens // 2]
    proj = acc[...]
    turned = pltpu.roll(proj, 64, 1)
    logit = dot_t(jnp.ones((8, 128), F32), lacc[...])
    kown[0:64, :] = jnp.where(low_half, turned[0:64], proj[64:128])
    kown[64:72, :] = 1.0 / (1.0 + jnp.exp(-logit))

    def k_copy(src, r, i, to):
        return remote(src, kbuf.at[r], k_send.at[i], k_recv.at[r], to)

    v_sib = remote(values, vbuf.at[s], d_send, d_recv, sib)

    @pl.when(first)
    def _():
        k_copy(kown, s, 0, sib).start()
        v_sib.start()

    @pl.when(s == 1)
    def _():
        k_copy(kown, 1, 0, cross).start()
        k_copy(kown, 0, 0, sib).wait_recv()
        k_copy(kbuf.at[0], 0, 1, cross).start()
        v_start(EARLY, chunks, 1)

    phi_q = phi_of(halves(proj, turned, low))

    def relay(k, slot):
        c = columns(k)
        b = vbuf.at[slot, :, c]
        return remote(b, b, r_send.at[k], r_recv.at[k], sib)

    def take(k, slot):
        v_copy(k, slot).wait_recv()
        relay(k, slot).start()

    pl.when(s == 2)(lambda: pl.loop(0, HALFWAY)(lambda k: take(k, 0)))
    pl.when(s == 3)(lambda: pl.loop(0, EARLY)(lambda k: take(k, 1)))

    @pl.when(s == 2)
    def _():
        for r in (1, 0):
            k_copy(kown, r, 0, sib).wait_recv()

    @pl.when(s == 3)
    def _():
        for i, r in enumerate((1, 0)):
            k_copy(kown, r, 0, cross).wait_recv()
            k_copy(kbuf.at[r], r, 1 + i, sib).start()
        k_copy(kown, 2, 0, sib).wait_recv()

    @pl.when(s > 0)
    def _():
        keeps, phis, betas, gains = [], [], [], []
        norm = jnp.zeros((1, 128 * NU), F32)
        for r in range(SEGS - 1):
            two = kbuf[r, 0:64, :]
            two_turned = pltpu.roll(two, 64, 1)
            p = jnp.concatenate(
                [halves(two, two_turned, low_half), halves(two_turned, two, low_half)], axis=0
            )
            phi = phi_of(p)
            beta = kbuf[r, 64:72, :]
            div = jnp.maximum(dot_t(jnp.broadcast_to(norm, (8, 128 * NU)), phi), 1.0)
            keep = jnp.where((idm[0, r + 1] == idm[0, r]) | (s < r + 1), 1.0, 0.0).astype(F32)
            phis.append(phi)
            betas.append(beta[0:1])
            gains.append((beta / div)[0:1])
            keeps.append(keep)
            norm = keep * (norm + jnp.sum(phi, axis=0, keepdims=True))
        scale = 1.0 / jnp.maximum(jnp.sum(phi_q * norm, axis=1, keepdims=True), 1.0)
        q = phi_q
        for r in reversed(range(SEGS - 1)):
            q = keeps[r] * q
            t = dot_t(q, phis[r])
            m = t * betas[r] * scale
            hi = m.astype(BF16)
            m_hi[:, 128 * r : 128 * (r + 1)] = hi
            m_lo[:, 128 * r : 128 * (r + 1)] = (m - hi.astype(F32)).astype(BF16)
            if r:
                q = q - dot(t * gains[r], phis[r])

    def mix(k, n):
        c = columns(k)
        v = vbuf[0:n, :, c].reshape(128 * n, CHUNK)
        mixed = jnp.dot(m_hi[:, : 128 * n], v, preferred_element_type=F32)
        mixed += jnp.dot(m_lo[:, : 128 * n], v, preferred_element_type=F32)
        out[:, c] = mixed.astype(BF16)

    @pl.when(s == 0)
    def _():
        out[...] = jnp.zeros_like(out)

    @pl.when(s == 1)
    def _():
        remote(values, vbuf.at[0], d_send, d_recv, sib).wait_recv()
        pl.loop(0, chunks)(lambda k: mix(k, 1))

    @pl.when(s == 2)
    def _():
        pl.loop(HALFWAY, chunks)(lambda k: take(k, 0))

        @pl.loop(0, chunks)
        def _(k):
            relay(k, 1).wait_recv()
            mix(k, 2)

        pl.loop(0, chunks)(lambda k: relay(k, 0).wait_send())

    @pl.when(s == 3)
    def _():
        remote(values, vbuf.at[2], d_send, d_recv, sib).wait_recv()

        @pl.loop(0, EARLY)
        def _(k):
            relay(k, 0).wait_recv()
            mix(k, 3)

        @pl.loop(EARLY, chunks)
        def _(k):
            take(k, 1)
            relay(k, 0).wait_recv()
            mix(k, 3)

        pl.loop(0, chunks)(lambda k: relay(k, 1).wait_send())

    @pl.when(first)
    def _():
        k_copy(kown, s, 0, sib).wait_send()
        v_sib.wait_send()

    @pl.when(second)
    def _():
        y_copy.wait_send()
        for c in (*x_copies, *sum(rings.values(), []), *(to_sib(i) for i in range(Z))):
            c.wait_send()

    @pl.when(s < 2)
    def _():
        pl.loop(0, chunks)(lambda k: v_copy(k, s).wait_send())

    @pl.when(s == 1)
    def _():
        k_copy(kown, 1, 0, cross).wait_send()
        k_copy(kbuf.at[0], 0, 1, cross).wait_send()

    @pl.when(s == 3)
    def _():
        for i, r in enumerate((1, 0)):
            k_copy(kbuf.at[r], r, 1 + i, sib).wait_send()


def per_device(hidden, value_states, w_in, w_beta, book_ids):
    _, tokens, width = hidden.shape
    chunks = width // CHUNK
    dma = pltpu.SemaphoreType.DMA
    hbm = pl.BlockSpec(memory_space=pltpu.HBM)
    mixed = pl.pallas_call(
        kernel,
        out_shape=jax.ShapeDtypeStruct((tokens, width), BF16),
        in_specs=[hbm] * 5,
        out_specs=pl.BlockSpec(memory_space=pltpu.VMEM),
        scratch_shapes=[
            pltpu.VMEM((tokens, width), BF16),
            pltpu.VMEM((Z, X, YL, 144, 128), BF16),
            pltpu.VMEM((SEGS - 1, tokens, width), BF16),
            pltpu.VMEM((72, 128), F32),
            pltpu.VMEM((SEGS - 1, 72, 128), F32),
            pltpu.VMEM((tokens, 128 * (SEGS - 1)), BF16),
            pltpu.VMEM((tokens, 128 * (SEGS - 1)), BF16),
            pltpu.VMEM((tokens, 128), F32),
            pltpu.VMEM((tokens, 128), F32),
            pltpu.VMEM((1, 128), BF16), pltpu.SMEM((1, SEGS), jnp.int32),
            dma, dma, dma, dma, dma, dma, dma((X - 1,)), dma((X - 1,)),
            dma((Z // 2, X)), dma((Z // 2, X)), dma((Z // 2, X)), dma((Z // 2, X)),
            dma((Z,)), dma((Z,)), dma((3,)), dma((SEGS - 1,)),
            dma((chunks,)), dma((chunks,)), dma((chunks,)), dma((chunks,)), dma, dma,
        ],
        compiler_params=pltpu.CompilerParams(
            collective_id=0, has_side_effects=True, vmem_limit_bytes=32 << 20
        ),
    )(*(
        pltpu.with_memory_space_constraint(a, pltpu.HBM)
        for a in (hidden[0], value_states[0], w_in, w_beta.reshape(1, 128), book_ids)
    ))
    return mixed[None]


def solution(mesh):
    return jax.shard_map(
        per_device,
        mesh=mesh,
        in_specs=(
            P("fsdp", "seg", None),
            P("fsdp", "seg", None),
            P("fsdp", None),
            P("fsdp"),
            P("fsdp", None),
        ),
        out_specs=P("fsdp", "seg", None),
        check_vma=False,
    )
```

```python
import functools

import jax
import jax.numpy as jnp
from jax import lax
from jax.experimental import pallas as pl
from jax.experimental.pallas import tpu as pltpu
from jax.sharding import PartitionSpec as P

NU = 3
X, Z, YL, SEGS = 4, 8, 2, 4
X_ORDER = (1, 3, 2)
GROUPS = ((0, 16, 512),)
CHUNKS = 16
EARLY = 8
HALFWAY = 8
MESH = pl.DeviceIdType.MESH
HIGHEST = lax.Precision.HIGHEST
F32, BF16 = jnp.float32, jnp.bfloat16


def dot(a, b):
    return jnp.dot(a, b, precision=HIGHEST, preferred_element_type=F32)


def dot_t(a, b):
    return lax.dot_general(
        a, b, (((1,), (1,)), ((), ())), precision=HIGHEST, preferred_element_type=F32
    )


def halves(u, turned, low):
    return jnp.where(low, jnp.maximum(u, 0.0), jnp.maximum(-turned, 0.0))


def phi_of(p):
    return jnp.concatenate([p * pltpu.roll(p, j, 1) for j in range(1, NU + 1)], axis=1)


def kernel(
    hidden, values, w_in, w_beta, ids, out,
    hid, wbuf, vbuf, kown, kbuf, m_hi, m_lo, acc, lacc,
    wb, idm, hid_sem, w_sem, wb_sem, id_sem, y_send, y_recv, x_send, x_recv, ring_send, zr_recv, zl_recv,
    s_send, s_recv, k_send, k_recv, v_send, v_recv, r_send, r_recv, d_send, d_recv,
):
    s, f = lax.axis_index("seg"), lax.axis_index("fsdp")
    core, yl = lax.rem(s, 2), lax.rem(f, YL)
    z = lax.rem(lax.div(f, YL), Z)
    x = lax.div(f, YL * Z)
    tokens = hid.shape[0]
    first, second = core == 0, core == 1

    def at(x_, z_, yl_):
        return (x_ * Z + z_) * YL + yl_

    sib = (s + 1 - 2 * core, f)
    cross = (lax.rem(s + 2, SEGS), f)
    y_peer = (s, at(x, z, 1 - yl))
    y_cross = (lax.rem(s + 2, SEGS), at(x, z, 1 - yl))
    x_peer = [(s, at(lax.rem(x + d, X), z, yl)) for d in X_ORDER]
    right = (s, at(x, lax.rem(z + 1, Z), yl))
    left = (s, at(x, lax.rem(z + Z - 1, Z), yl))

    def remote(src, dst, send, recv, to):
        return pltpu.make_async_remote_copy(
            src_ref=src, dst_ref=dst, send_sem=send, recv_sem=recv, device_id=to, device_id_type=MESH
        )

    barrier = pltpu.get_barrier_semaphore()
    near, far = [cross, sib], [y_cross, *x_peer, right, left]

    def greet(peers):
        for peer in peers:
            pl.semaphore_signal(barrier, inc=1, device_id=peer, device_id_type=MESH)

    greet(near)
    pl.when(second)(lambda: greet(far))
    pl.when(s == 3)(lambda: greet([y_peer]))
    hid_copy = pltpu.make_async_copy(hidden, hid, hid_sem)
    w_copy = pltpu.make_async_copy(w_in, wbuf.at[z, x, yl, pl.ds(0, 128)], w_sem)
    wb_copy = pltpu.make_async_copy(w_beta, wb, wb_sem)
    id_copy = pltpu.make_async_copy(ids, idm, id_sem)

    @pl.when(second)
    def _():
        w_copy.start()
        wb_copy.start()

    hid_copy.start()
    id_copy.start()
    for r in range(SEGS - 1):

        @pl.when(s <= r)
        def _(r=r):
            kbuf[r] = jnp.zeros(kbuf.shape[1:], BF16)

    def each(lo, hi, body):
        for start, count, wide in GROUPS:
            col0 = sum(min(max(start - a, 0), n) * w for a, n, w in GROUPS)
            a, b = max(lo, start), min(hi, start + count)
            if a < b:

                @pl.loop(a, b)
                def _(k):
                    body(k, pl.ds(pl.multiple_of(col0 + (k - start) * wide, 256), wide), wide)

    def v_copy(k, c, slot):
        return remote(values.at[:, c], vbuf.at[slot, :, c], v_send, v_recv.at[k], cross)

    def v_start(lo, hi, slot):
        each(lo, hi, lambda k, c, _: v_copy(k, c, slot).start())

    def project(zb):
        total = jnp.zeros((tokens, 128), F32)
        gate = jnp.zeros((tokens, 128), F32)
        for xb in range(X):
            lo = pl.multiple_of(at(xb, zb, 0) * 128, 128 * YL)
            h = hid[:, pl.ds(lo, 128 * YL)]
            w = jnp.concatenate([wbuf[zb, xb, p, 0:128, :] for p in range(YL)], axis=0)
            total += jnp.dot(h, w, preferred_element_type=F32)
            for p in range(YL):
                row = wbuf[zb, xb, p, 128:144, :][0:1].astype(F32)
                gate += h[:, 128 * p : 128 * (p + 1)].astype(F32) * row
        acc[...] += total
        lacc[...] += gate

    def block(d):
        return lax.rem(z + d + Z, Z)

    half = Z // 2
    order = [0] + [d for t in range(1, half) for d in (-t, t)] + [half]

    def to_sib(i):
        b = wbuf.at[block(order[i])]
        return remote(b, b, s_send, s_recv.at[(i + 1) // 2], sib)

    def took(n, sem):
        b = wbuf.at[pl.ds(0, n)]
        remote(b, b, s_send, s_recv.at[sem], sib).wait_recv()

    def clear():
        acc[...] = jnp.zeros_like(acc)
        lacc[...] = jnp.zeros_like(lacc)
        hid_copy.wait()
        id_copy.wait()

    own, pair = wbuf.at[z, x, yl], wbuf.at[z, x]
    y_copies = [remote(own, own, y_send, y_recv, to) for to in (y_peer, y_cross)]
    x_copies = [remote(pair, pair, x_send, x_recv, peer) for peer in x_peer]

    def ring(t, j):
        xs, g = lax.rem(x + X - (0, *X_ORDER)[j], X), min(j, 1)
        if t < half or j < X // 2:
            b = wbuf.at[block(1 - t), xs]
            remote(b, b, ring_send, zr_recv.at[t - 1, g], right).start()
        if t < half or j >= X // 2:
            b = wbuf.at[block(t - 1), xs]
            remote(b, b, ring_send, zl_recv.at[t - 1, g], left).start()

    def came(t, g):
        for sem, n in (
            (zr_recv, (1, 3)[g] if t < half else 1),
            (zl_recv, (1, 3)[g] if t < half else 2 * g),
        ):
            if n:
                b = wbuf.at[0, pl.ds(0, n)]
                remote(b, b, ring_send, sem.at[t - 1, g], left).wait_recv()

    @pl.when(first)
    def _():
        pl.semaphore_wait(barrier, len(near))
        pl.when(s == 0)(lambda: v_start(0, CHUNKS, 0))
        clear()
        for sem in range(half + 1):
            blocks = [i for i in range(Z) if (i + 1) // 2 == sem]
            took(len(blocks), sem)
            for i in blocks:
                project(block(order[i]))

    @pl.when(second)
    def _():
        wb_copy.wait()
        wbuf[z, x, yl, 128:144, :] = jnp.broadcast_to(wb[...], (16, 128))
        w_copy.wait()

        @pl.when(s == 1)
        def _():
            pl.semaphore_wait(barrier, len(near) + len(far))
            v_start(0, EARLY, 1)

        @pl.when(s == 3)
        def _():
            pl.semaphore_wait(barrier, len(near) + len(far) + 1)
            for c in y_copies:
                c.start()

        y_copies[0].wait_recv()
        for c in x_copies:
            c.start()
        ring(1, 0)
        clear()
        b = wbuf.at[0, pl.ds(0, X - 1)]
        remote(b, b, x_send, x_recv, sib).wait_recv()
        for j in range(1, X):
            ring(1, j)
        to_sib(0).start()
        project(block(0))
        for t in range(1, half + 1):
            for g in range(2):
                came(t, g)
                if t < half:
                    for j in ((0,), (1, 2, 3))[g]:
                        ring(t + 1, j)
            fresh = [i for i in (2 * t - 1, 2 * t) if i < Z]
            for i in fresh:
                to_sib(i).start()
            for i in fresh:
                project(block(order[i]))

    low = lax.broadcasted_iota(jnp.int32, (tokens, 128), 1) < 64
    low_half = low[: tokens // 2]
    proj = acc[...]
    turned = pltpu.roll(proj, 64, 1)
    logit = dot_t(jnp.ones((8, 128), F32), lacc[...])
    gate = 1.0 / (1.0 + jnp.exp(-logit))
    gate_hi = gate.astype(BF16)
    gate_lo = (gate - gate_hi.astype(F32)).astype(BF16)
    kown[0:64, :] = jnp.where(low_half, turned[0:64], proj[64:128]).astype(BF16)
    kown[64:80, :] = jnp.concatenate([gate_hi, gate_lo], axis=0)

    def k_copy(src, r, to):
        return remote(src, kbuf.at[r], k_send, k_recv.at[r], to)

    v_sib = remote(values, vbuf.at[s], d_send, d_recv, sib)

    @pl.when(first)
    def _():
        k_copy(kown, s, sib).start()
        v_sib.start()

    @pl.when(s == 1)
    def _():
        k_copy(kown, 1, cross).start()
        k_copy(kown, 0, sib).wait_recv()
        k_copy(kbuf.at[0], 0, cross).start()
        v_start(EARLY, CHUNKS, 1)

    phi_q = phi_of(halves(proj, turned, low))

    def relay(k, c, slot):
        b = vbuf.at[slot, :, c]
        return remote(b, b, r_send, r_recv.at[k], sib)

    def take(k, c, slot):
        v_copy(k, c, slot).wait_recv()
        relay(k, c, slot).start()

    pl.when(s == 2)(lambda: each(0, HALFWAY, lambda k, c, _: take(k, c, 0)))
    pl.when(s == 3)(lambda: each(0, EARLY, lambda k, c, _: take(k, c, 1)))

    @pl.when(s == 2)
    def _():
        for r in (1, 0):
            k_copy(kown, r, sib).wait_recv()

    @pl.when(s == 3)
    def _():
        for r in (1, 0):
            k_copy(kown, r, cross).wait_recv()
            k_copy(kbuf.at[r], r, sib).start()
        k_copy(kown, 2, sib).wait_recv()

    @pl.when(s > 0)
    def _():
        keeps, phis, betas, gains = [], [], [], []
        norm = jnp.zeros((1, 128 * NU), F32)
        for r in range(SEGS - 1):
            two = kbuf[r, 0:64, :].astype(F32)
            two_turned = pltpu.roll(two, 64, 1)
            p = jnp.concatenate(
                [halves(two, two_turned, low_half), halves(two_turned, two, low_half)], axis=0
            )
            phi = phi_of(p)
            gates = kbuf[r, 64:80, :].astype(F32)
            beta = gates[0:8] + gates[8:16]
            div = jnp.maximum(dot_t(jnp.broadcast_to(norm, (8, 128 * NU)), phi), 1.0)
            keep = jnp.where((idm[0, r + 1] == idm[0, r]) | (s < r + 1), 1.0, 0.0).astype(F32)
            phis.append(phi)
            betas.append(beta[0:1])
            gains.append((beta / div)[0:1])
            keeps.append(keep)
            norm = keep * (norm + jnp.sum(phi, axis=0, keepdims=True))
        scale = 1.0 / jnp.maximum(jnp.sum(phi_q * norm, axis=1, keepdims=True), 1.0)
        q = phi_q
        for r in reversed(range(SEGS - 1)):
            q = keeps[r] * q
            t = dot_t(q, phis[r])
            m = t * betas[r] * scale
            hi = m.astype(BF16)
            m_hi[:, 128 * r : 128 * (r + 1)] = hi
            m_lo[:, 128 * r : 128 * (r + 1)] = (m - hi.astype(F32)).astype(BF16)
            if r:
                q = q - dot(t * gains[r], phis[r])

    def mix(c, wide, n):
        v = vbuf[0:n, :, c].reshape(128 * n, wide)
        mixed = jnp.dot(m_hi[:, : 128 * n], v, preferred_element_type=F32)
        mixed += jnp.dot(m_lo[:, : 128 * n], v, preferred_element_type=F32)
        out[:, c] = mixed.astype(BF16)

    @pl.when(s == 0)
    def _():
        out[...] = jnp.zeros_like(out)

    @pl.when(s == 1)
    def _():
        remote(values, vbuf.at[0], d_send, d_recv, sib).wait_recv()
        each(0, CHUNKS, lambda k, c, wide: mix(c, wide, 1))

    def last(slot, n, taken):
        def use(k, c, wide):
            relay(k, c, 1 - slot).wait_recv()
            mix(c, wide, n)

        def take_use(k, c, wide):
            take(k, c, slot)
            use(k, c, wide)

        each(0, taken, use)
        each(taken, CHUNKS, take_use)
        relay(0, slice(None), slot).wait_send()

    @pl.when(s == 2)
    def _():
        last(0, 2, HALFWAY)

    @pl.when(s == 3)
    def _():
        remote(values, vbuf.at[2], d_send, d_recv, sib).wait_recv()
        last(1, 3, EARLY)

    @pl.when(first)
    def _():
        k_copy(kown, s, sib).wait_send()
        v_sib.wait_send()

    @pl.when(second)
    def _():
        for n, sem in ((Z - 1, ring_send), (Z, s_send)):
            b = wbuf.at[pl.ds(0, n)]
            remote(b, b, sem, s_recv.at[0], sib).wait_send()
        b = wbuf.at[0, pl.ds(0, X - 1)]
        remote(b, b, x_send, x_recv, sib).wait_send()
        b = kbuf.at[pl.ds(0, 2)]
        remote(b, b, k_send, k_recv.at[0], sib).wait_send()

    @pl.when(s == 3)
    def _():
        remote(pair, pair, y_send, y_recv, sib).wait_send()

    @pl.when(s < 2)
    def _():
        remote(values, vbuf.at[0], v_send, v_recv.at[0], cross).wait_send()


def per_device(hidden, value_states, w_in, w_beta, book_ids):
    _, tokens, width = hidden.shape
    dma = pltpu.SemaphoreType.DMA
    hbm = pl.BlockSpec(memory_space=pltpu.HBM)
    mixed = pl.pallas_call(
        kernel,
        out_shape=jax.ShapeDtypeStruct((tokens, width), BF16),
        in_specs=[hbm] * 5,
        out_specs=pl.BlockSpec(memory_space=pltpu.VMEM),
        scratch_shapes=[
            pltpu.VMEM((tokens, width), BF16),
            pltpu.VMEM((Z, X, YL, 144, 128), BF16),
            pltpu.VMEM((SEGS - 1, tokens, width), BF16),
            pltpu.VMEM((80, 128), BF16),
            pltpu.VMEM((SEGS - 1, 80, 128), BF16),
            pltpu.VMEM((tokens, 128 * (SEGS - 1)), BF16),
            pltpu.VMEM((tokens, 128 * (SEGS - 1)), BF16),
            pltpu.VMEM((tokens, 128), F32),
            pltpu.VMEM((tokens, 128), F32),
            pltpu.VMEM((1, 128), BF16), pltpu.SMEM((1, SEGS), jnp.int32),
            dma, dma, dma, dma, dma, dma, dma, dma, dma, dma((Z // 2, 2)), dma((Z // 2, 2)),
            dma, dma((Z // 2 + 1,)), dma, dma((SEGS - 1,)),
            dma, dma((CHUNKS,)), dma, dma((CHUNKS,)), dma, dma,
        ],
        compiler_params=pltpu.CompilerParams(
            collective_id=0, has_side_effects=True, vmem_limit_bytes=32 << 20
        ),
    )(*(
        pltpu.with_memory_space_constraint(a, pltpu.HBM)
        for a in (hidden[0], value_states[0], w_in, w_beta.reshape(1, 128), book_ids)
    ))
    return mixed[None]


def solution(mesh):
    return jax.shard_map(
        per_device,
        mesh=mesh,
        in_specs=(
            P("fsdp", "seg", None),
            P("fsdp", "seg", None),
            P("fsdp", None),
            P("fsdp"),
            P("fsdp", None),
        ),
        out_specs=P("fsdp", "seg", None),
        check_vma=False,
    )
```

```python
import functools

import jax
import jax.numpy as jnp
from jax import lax
from jax.experimental import pallas as pl
from jax.experimental.pallas import tpu as pltpu
from jax.sharding import PartitionSpec as P

NU = 3
X, Z, YL, SEGS = 4, 8, 2, 4
X_ORDER = (1, 3, 2)
GROUPS = ((0, 16, 512),)
CHUNKS = 16
EARLY = 10
HALFWAY = 8
MESH = pl.DeviceIdType.MESH
HIGHEST = lax.Precision.HIGHEST
F32, BF16 = jnp.float32, jnp.bfloat16


def dot(a, b):
    return jnp.dot(a, b, precision=HIGHEST, preferred_element_type=F32)


def dot_t(a, b):
    return lax.dot_general(
        a, b, (((1,), (1,)), ((), ())), precision=HIGHEST, preferred_element_type=F32
    )


def halves(u, turned, low):
    return jnp.where(low, jnp.maximum(u, 0.0), jnp.maximum(-turned, 0.0))


def phi_of(p):
    return jnp.concatenate([p * pltpu.roll(p, j, 1) for j in range(1, NU + 1)], axis=1)


def kernel(
    hidden, values, w_in, w_beta, ids, out,
    hid, wbuf, vbuf, kown, kbuf, mats, acc, lacc,
    wb, idm, ready, go, hid_sem, w_sem, wb_sem, id_sem, y_send, y_recv, x_send, x_recv, ring_send, zr_recv, zl_recv,
    s_send, s_recv, k_send, k_recv, v_send, v_recv, r_send, r_recv, d_send, d_recv,
):
    s, f = lax.axis_index("seg"), lax.axis_index("fsdp")
    core, yl = lax.rem(s, 2), lax.rem(f, YL)
    z = lax.rem(lax.div(f, YL), Z)
    x = lax.div(f, YL * Z)
    tokens = hid.shape[0]
    first, second = core == 0, core == 1

    def at(x_, z_, yl_):
        return (x_ * Z + z_) * YL + yl_

    sib = (s + 1 - 2 * core, f)
    cross = (lax.rem(s + 2, SEGS), f)
    y_peer = (s, at(x, z, 1 - yl))
    y_cross = (lax.rem(s + 2, SEGS), at(x, z, 1 - yl))
    x_peer = [(s, at(lax.rem(x + d, X), z, yl)) for d in X_ORDER]
    right = (s, at(x, lax.rem(z + 1, Z), yl))
    left = (s, at(x, lax.rem(z + Z - 1, Z), yl))

    def remote(src, dst, send, recv, to):
        return pltpu.make_async_remote_copy(
            src_ref=src, dst_ref=dst, send_sem=send, recv_sem=recv, device_id=to, device_id_type=MESH
        )

    barrier = pltpu.get_barrier_semaphore()
    near, far = [cross, sib], [y_peer, *x_peer, right, left]

    def greet(peers):
        for peer in peers:
            pl.semaphore_signal(barrier, inc=1, device_id=peer, device_id_type=MESH)

    greet(near)
    pl.when(s == 3)(lambda: greet(far))
    hid_copy = pltpu.make_async_copy(hidden, hid, hid_sem)
    w_copy = pltpu.make_async_copy(w_in, wbuf.at[z, x, yl, pl.ds(0, 128)], w_sem)
    wb_copy = pltpu.make_async_copy(w_beta, wb, wb_sem)
    id_copy = pltpu.make_async_copy(ids, idm, id_sem)

    @pl.when(second)
    def _():
        w_copy.start()
        wb_copy.start()

    hid_copy.start()
    id_copy.start()
    for r in range(SEGS - 1):

        @pl.when(s <= r)
        def _(r=r):
            kbuf[r] = jnp.zeros(kbuf.shape[1:], BF16)

    def each(lo, hi, body):
        for start, count, wide in GROUPS:
            col0 = sum(min(max(start - a, 0), n) * w for a, n, w in GROUPS)
            a, b = max(lo, start), min(hi, start + count)
            if a < b:

                @pl.loop(a, b)
                def _(k):
                    body(k, pl.ds(pl.multiple_of(col0 + (k - start) * wide, 256), wide), wide)

    def v_copy(k, c, slot):
        return remote(values.at[:, c], vbuf.at[slot, :, c], v_send, v_recv.at[k], cross)

    def v_start(lo, hi, slot):
        each(lo, hi, lambda k, c, _: v_copy(k, c, slot).start())

    def project(zb):
        total = jnp.zeros((tokens, 128), F32)
        gate = jnp.zeros((tokens, 128), F32)
        for xb in range(X):
            lo = pl.multiple_of(at(xb, zb, 0) * 128, 128 * YL)
            h = hid[:, pl.ds(lo, 128 * YL)]
            w = jnp.concatenate([wbuf[zb, xb, p, 0:128, :] for p in range(YL)], axis=0)
            total += jnp.dot(h, w, preferred_element_type=F32)
            for p in range(YL):
                row = wbuf[zb, xb, p, 128:144, :][0:1].astype(F32)
                gate += h[:, 128 * p : 128 * (p + 1)].astype(F32) * row
        acc[...] += total
        lacc[...] += gate

    def block(d):
        return lax.rem(z + d + Z, Z)

    half = Z // 2
    order = [0] + [d for t in range(1, half) for d in (-t, t)] + [half]

    def to_sib(i):
        b = wbuf.at[block(order[i])]
        return remote(b, b, s_send, s_recv.at[(i + 1) // 2], sib)

    def took(n, sem):
        b = wbuf.at[pl.ds(0, n)]
        remote(b, b, s_send, s_recv.at[sem], sib).wait_recv()

    def clear():
        acc[...] = jnp.zeros_like(acc)
        lacc[...] = jnp.zeros_like(lacc)
        hid_copy.wait()
        id_copy.wait()

    own, pair = wbuf.at[z, x, yl], wbuf.at[z, x]
    y_copies = [remote(own, own, y_send, y_recv, to) for to in (y_peer, y_cross)]
    x_copies = [remote(pair, pair, x_send, x_recv, peer) for peer in x_peer]

    def ring(t, j):
        xs, g = lax.rem(x + X - (0, *X_ORDER)[j], X), min(j, 1)
        if t < half or j < X // 2:
            b = wbuf.at[block(1 - t), xs]
            remote(b, b, ring_send, zr_recv.at[t - 1, g], right).start()
        if t < half or j >= X // 2:
            b = wbuf.at[block(t - 1), xs]
            remote(b, b, ring_send, zl_recv.at[t - 1, g], left).start()

    def came(t, g):
        for sem, n in (
            (zr_recv, (1, 3)[g] if t < half else 1),
            (zl_recv, (1, 3)[g] if t < half else 2 * g),
        ):
            if n:
                b = wbuf.at[0, pl.ds(0, n)]
                remote(b, b, ring_send, sem.at[t - 1, g], left).wait_recv()

    @pl.when(first)
    def _():
        pl.semaphore_wait(barrier, len(near))
        pl.when(s == 0)(lambda: v_start(0, CHUNKS, 0))
        clear()
        for sem in range(half + 1):
            blocks = [i for i in range(Z) if (i + 1) // 2 == sem]
            took(len(blocks), sem)
            for i in blocks:
                project(block(order[i]))

    @pl.when(second)
    def _():
        wb_copy.wait()
        wbuf[z, x, yl, 128:144, :] = jnp.broadcast_to(wb[...], (16, 128))
        w_copy.wait()

        @pl.when(s == 1)
        def _():
            pl.semaphore_wait(barrier, len(near))
            v_start(0, EARLY, 1)
            pl.semaphore_wait(go, 1)

        @pl.when(s == 3)
        def _():
            pl.semaphore_wait(barrier, len(near) + len(far))
            y_copies[0].start()
            for peer in far:
                pl.semaphore_signal(ready, inc=1, device_id=peer, device_id_type=MESH)
            pl.semaphore_wait(ready, len(far))
            pl.semaphore_signal(go, inc=1, device_id=cross, device_id_type=MESH)
            y_copies[1].start()

        y_copies[0].wait_recv()
        for c in x_copies:
            c.start()
        ring(1, 0)
        clear()
        b = wbuf.at[0, pl.ds(0, X - 1)]
        remote(b, b, x_send, x_recv, sib).wait_recv()
        for j in range(1, X):
            ring(1, j)
        to_sib(0).start()
        project(block(0))
        for t in range(1, half + 1):
            for g in range(2):
                came(t, g)
                if t < half:
                    for j in ((0,), (1, 2, 3))[g]:
                        ring(t + 1, j)
            fresh = [i for i in (2 * t - 1, 2 * t) if i < Z]
            for i in fresh:
                to_sib(i).start()
            for i in fresh:
                project(block(order[i]))

    low = lax.broadcasted_iota(jnp.int32, (tokens, 128), 1) < 64
    low_half = low[: tokens // 2]
    proj = acc[...]
    turned = pltpu.roll(proj, 64, 1)
    logit = dot_t(jnp.ones((8, 128), F32), lacc[...])
    gate = 1.0 / (1.0 + jnp.exp(-logit))
    gate_hi = gate.astype(BF16)
    gate_lo = (gate - gate_hi.astype(F32)).astype(BF16)
    kown[0:64, :] = jnp.where(low_half, turned[0:64], proj[64:128]).astype(BF16)
    kown[64:80, :] = jnp.concatenate([gate_hi, gate_lo], axis=0)

    def k_copy(src, r, to):
        return remote(src, kbuf.at[r], k_send, k_recv.at[r], to)

    v_sib = remote(values, vbuf.at[s], d_send, d_recv, sib)

    @pl.when(first)
    def _():
        k_copy(kown, s, sib).start()
        v_sib.start()

    @pl.when(s == 1)
    def _():
        k_copy(kown, 1, cross).start()
        k_copy(kown, 0, sib).wait_recv()
        k_copy(kbuf.at[0], 0, cross).start()
        v_start(EARLY, CHUNKS, 1)

    phi_q = phi_of(halves(proj, turned, low))

    def relay(k, c, slot):
        b = vbuf.at[slot, :, c]
        return remote(b, b, r_send, r_recv.at[k], sib)

    def take(k, c, slot):
        v_copy(k, c, slot).wait_recv()
        relay(k, c, slot).start()

    pl.when(s == 2)(lambda: each(0, HALFWAY, lambda k, c, _: take(k, c, 0)))
    pl.when(s == 3)(lambda: each(0, EARLY, lambda k, c, _: take(k, c, 1)))

    @pl.when(s == 2)
    def _():
        for r in (1, 0):
            k_copy(kown, r, sib).wait_recv()

    @pl.when(s == 3)
    def _():
        for r in (1, 0):
            k_copy(kown, r, cross).wait_recv()
            k_copy(kbuf.at[r], r, sib).start()
        k_copy(kown, 2, sib).wait_recv()

    @pl.when(s > 0)
    def _():
        keeps, phis, betas, gains = [], [], [], []
        norm = jnp.zeros((1, 128 * NU), F32)
        for r in range(SEGS - 1):
            two = kbuf[r, 0:64, :].astype(F32)
            two_turned = pltpu.roll(two, 64, 1)
            p = jnp.concatenate(
                [halves(two, two_turned, low_half), halves(two_turned, two, low_half)], axis=0
            )
            phi = phi_of(p)
            gates = kbuf[r, 64:80, :].astype(F32)
            beta = gates[0:8] + gates[8:16]
            div = jnp.maximum(dot_t(jnp.broadcast_to(norm, (8, 128 * NU)), phi), 1.0)
            keep = jnp.where((idm[0, r + 1] == idm[0, r]) | (s < r + 1), 1.0, 0.0).astype(F32)
            phis.append(phi)
            betas.append(beta[0:1])
            gains.append((beta / div)[0:1])
            keeps.append(keep)
            norm = keep * (norm + jnp.sum(phi, axis=0, keepdims=True))
        scale = 1.0 / jnp.maximum(jnp.sum(phi_q * norm, axis=1, keepdims=True), 1.0)
        q = phi_q
        for r in reversed(range(SEGS - 1)):
            q = keeps[r] * q
            t = dot_t(q, phis[r])
            m = t * betas[r] * scale
            mats[:, 128 * r : 128 * (r + 1)] = m.astype(BF16)
            if r:
                q = q - dot(t * gains[r], phis[r])

    def mix(c, wide, n):
        v = vbuf[0:n, :, c].reshape(128 * n, wide)
        mixed = jnp.dot(mats[:, : 128 * n], v, preferred_element_type=F32)
        out[:, c] = mixed.astype(BF16)

    @pl.when(s == 0)
    def _():
        out[...] = jnp.zeros_like(out)

    @pl.when(s == 1)
    def _():
        remote(values, vbuf.at[0], d_send, d_recv, sib).wait_recv()
        each(0, CHUNKS, lambda k, c, wide: mix(c, wide, 1))

    def last(slot, n, taken):
        def use(k, c, wide):
            relay(k, c, 1 - slot).wait_recv()
            mix(c, wide, n)

        def take_use(k, c, wide):
            take(k, c, slot)
            use(k, c, wide)

        each(0, taken, use)
        each(taken, CHUNKS, take_use)
        relay(0, slice(None), slot).wait_send()

    @pl.when(s == 2)
    def _():
        last(0, 2, HALFWAY)

    @pl.when(s == 3)
    def _():
        remote(values, vbuf.at[2], d_send, d_recv, sib).wait_recv()
        last(1, 3, EARLY)

    @pl.when(first)
    def _():
        k_copy(kown, s, sib).wait_send()
        v_sib.wait_send()

    @pl.when(second)
    def _():
        for n, sem in ((Z - 1, ring_send), (Z, s_send)):
            b = wbuf.at[pl.ds(0, n)]
            remote(b, b, sem, s_recv.at[0], sib).wait_send()
        b = wbuf.at[0, pl.ds(0, X - 1)]
        remote(b, b, x_send, x_recv, sib).wait_send()
        b = kbuf.at[pl.ds(0, 2)]
        remote(b, b, k_send, k_recv.at[0], sib).wait_send()

    @pl.when(s == 3)
    def _():
        remote(pair, pair, y_send, y_recv, sib).wait_send()

    @pl.when(s < 2)
    def _():
        remote(values, vbuf.at[0], v_send, v_recv.at[0], cross).wait_send()


def per_device(hidden, value_states, w_in, w_beta, book_ids):
    _, tokens, width = hidden.shape
    dma = pltpu.SemaphoreType.DMA
    hbm = pl.BlockSpec(memory_space=pltpu.HBM)
    mixed = pl.pallas_call(
        kernel,
        out_shape=jax.ShapeDtypeStruct((tokens, width), BF16),
        in_specs=[hbm] * 5,
        out_specs=pl.BlockSpec(memory_space=pltpu.VMEM),
        scratch_shapes=[
            pltpu.VMEM((tokens, width), BF16),
            pltpu.VMEM((Z, X, YL, 144, 128), BF16),
            pltpu.VMEM((SEGS - 1, tokens, width), BF16),
            pltpu.VMEM((80, 128), BF16),
            pltpu.VMEM((SEGS - 1, 80, 128), BF16),
            pltpu.VMEM((tokens, 128 * (SEGS - 1)), BF16),
            pltpu.VMEM((tokens, 128), F32),
            pltpu.VMEM((tokens, 128), F32),
            pltpu.VMEM((1, 128), BF16), pltpu.SMEM((1, SEGS), jnp.int32),
            pltpu.SemaphoreType.REGULAR, pltpu.SemaphoreType.REGULAR,
            dma, dma, dma, dma, dma, dma, dma, dma, dma, dma((Z // 2, 2)), dma((Z // 2, 2)),
            dma, dma((Z // 2 + 1,)), dma, dma((SEGS - 1,)),
            dma, dma((CHUNKS,)), dma, dma((CHUNKS,)), dma, dma,
        ],
        compiler_params=pltpu.CompilerParams(
            collective_id=0, has_side_effects=True, vmem_limit_bytes=32 << 20
        ),
    )(*(
        pltpu.with_memory_space_constraint(a, pltpu.HBM)
        for a in (hidden[0], value_states[0], w_in, w_beta.reshape(1, 128), book_ids)
    ))
    return mixed[None]


def solution(mesh):
    return jax.shard_map(
        per_device,
        mesh=mesh,
        in_specs=(
            P("fsdp", "seg", None),
            P("fsdp", "seg", None),
            P("fsdp", None),
            P("fsdp"),
            P("fsdp", None),
        ),
        out_specs=P("fsdp", "seg", None),
        check_vma=False,
    )
```

```python
import functools

import jax
import jax.numpy as jnp
from jax import lax
from jax.experimental import pallas as pl
from jax.experimental.pallas import tpu as pltpu
from jax.sharding import PartitionSpec as P

NU = 3
X, Z, YL, SEGS = 4, 8, 2, 4
X_ORDER = (1, 3, 2)
GROUPS = ((0, 1, 4096), (1, 8, 512))
CHUNKS = 9
EARLY = 2
HALFWAY = 2
STEP = 512
MESH = pl.DeviceIdType.MESH
F32, BF16 = jnp.float32, jnp.bfloat16


def parts(a):
    high = a.astype(BF16)
    return high, (a - high.astype(F32)).astype(BF16)


def dot(a, b, dims=(((1,), (0,)), ((), ()))):
    (a_hi, a_lo), (b_hi, b_lo) = parts(a), parts(b)

    def one(x, y):
        return lax.dot_general(x, y, dims, preferred_element_type=F32)

    return one(a_hi, b_hi) + (one(a_hi, b_lo) + one(a_lo, b_hi))


def dot_t(a, b):
    return dot(a, b, (((1,), (1,)), ((), ())))


def halves(u, turned, low):
    return jnp.where(low, jnp.maximum(u, 0.0), jnp.maximum(-turned, 0.0))


def phi_of(p):
    return jnp.concatenate([p * pltpu.roll(p, j, 1) for j in range(1, NU + 1)], axis=1)


def kernel(
    hidden, values, w_in, w_beta, ids, out,
    hid, wbuf, vbuf, kown, kbuf, mats, acc, lacc,
    wb, idm, ready, go, hid_sem, w_sem, wb_sem, id_sem, y_send, y_recv, x_send, x_recv, ring_send, zr_recv, zl_recv,
    s_send, s_recv, k_send, k_recv, v_send, v_recv, r_send, r_recv, d_send, d_recv,
):
    s, f = lax.axis_index("seg"), lax.axis_index("fsdp")
    core, yl = lax.rem(s, 2), lax.rem(f, YL)
    z = lax.rem(lax.div(f, YL), Z)
    x = lax.div(f, YL * Z)
    tokens = hid.shape[0]
    first, second = core == 0, core == 1

    def at(x_, z_, yl_):
        return (x_ * Z + z_) * YL + yl_

    sib = (s + 1 - 2 * core, f)
    cross = (lax.rem(s + 2, SEGS), f)
    y_peer = (s, at(x, z, 1 - yl))
    y_cross = (lax.rem(s + 2, SEGS), at(x, z, 1 - yl))
    x_peer = [(s, at(lax.rem(x + d, X), z, yl)) for d in X_ORDER]
    right = (s, at(x, lax.rem(z + 1, Z), yl))
    left = (s, at(x, lax.rem(z + Z - 1, Z), yl))

    def remote(src, dst, send, recv, to):
        return pltpu.make_async_remote_copy(
            src_ref=src, dst_ref=dst, send_sem=send, recv_sem=recv, device_id=to, device_id_type=MESH
        )

    barrier = pltpu.get_barrier_semaphore()
    near, far = [cross, sib], [y_peer, *x_peer, right, left]

    def greet(peers):
        for peer in peers:
            pl.semaphore_signal(barrier, inc=1, device_id=peer, device_id_type=MESH)

    greet(near)
    pl.when(s == 3)(lambda: greet(far))
    hid_copy = pltpu.make_async_copy(hidden, hid, hid_sem)
    w_copy = pltpu.make_async_copy(w_in, wbuf.at[z, x, yl, pl.ds(0, 128)], w_sem)
    wb_copy = pltpu.make_async_copy(w_beta, wb, wb_sem)
    id_copy = pltpu.make_async_copy(ids, idm, id_sem)

    @pl.when(second)
    def _():
        w_copy.start()
        wb_copy.start()

    hid_copy.start()
    id_copy.start()
    for r in range(SEGS - 1):

        @pl.when(s <= r)
        def _(r=r):
            kbuf[r] = jnp.zeros(kbuf.shape[1:], BF16)

    def each(lo, hi, body):
        for start, count, wide in GROUPS:
            col0 = sum(min(max(start - a, 0), n) * w for a, n, w in GROUPS)
            a, b = max(lo, start), min(hi, start + count)
            if a < b:

                @pl.loop(a, b)
                def _(k):
                    body(k, pl.ds(pl.multiple_of(col0 + (k - start) * wide, 256), wide), wide)

    def v_copy(k, c, slot):
        return remote(values.at[:, c], vbuf.at[slot, :, c], v_send, v_recv.at[k], cross)

    def v_start(lo, hi, slot):
        each(lo, hi, lambda k, c, _: v_copy(k, c, slot).start())

    def project(zb):
        total = jnp.zeros((tokens, 128), F32)
        gate = jnp.zeros((tokens, 128), F32)
        for xb in range(X):
            lo = pl.multiple_of(at(xb, zb, 0) * 128, 128 * YL)
            h = hid[:, pl.ds(lo, 128 * YL)]
            w = jnp.concatenate([wbuf[zb, xb, p, 0:128, :] for p in range(YL)], axis=0)
            total += jnp.dot(h, w, preferred_element_type=F32)
            for p in range(YL):
                row = wbuf[zb, xb, p, 128:144, :][0:1].astype(F32)
                gate += h[:, 128 * p : 128 * (p + 1)].astype(F32) * row
        acc[...] += total
        lacc[...] += gate

    def block(d):
        return lax.rem(z + d + Z, Z)

    half = Z // 2
    order = [0] + [d for t in range(1, half) for d in (-t, t)] + [half]

    def to_sib(i):
        b = wbuf.at[block(order[i])]
        return remote(b, b, s_send, s_recv.at[(i + 1) // 2], sib)

    def took(n, sem):
        b = wbuf.at[pl.ds(0, n)]
        remote(b, b, s_send, s_recv.at[sem], sib).wait_recv()

    def clear():
        acc[...] = jnp.zeros_like(acc)
        lacc[...] = jnp.zeros_like(lacc)
        hid_copy.wait()
        id_copy.wait()

    own, pair = wbuf.at[z, x, yl], wbuf.at[z, x]
    y_copies = [remote(own, own, y_send, y_recv, to) for to in (y_peer, y_cross)]
    x_copies = [remote(pair, pair, x_send, x_recv, peer) for peer in x_peer]

    def ring(t, j):
        xs, g = lax.rem(x + X - (0, *X_ORDER)[j], X), min(j, 1)
        if t < half or j < X // 2:
            b = wbuf.at[block(1 - t), xs]
            remote(b, b, ring_send, zr_recv.at[t - 1, g], right).start()
        if t < half or j >= X // 2:
            b = wbuf.at[block(t - 1), xs]
            remote(b, b, ring_send, zl_recv.at[t - 1, g], left).start()

    def came(t, g):
        for sem, n in (
            (zr_recv, (1, 3)[g] if t < half else 1),
            (zl_recv, (1, 3)[g] if t < half else 2 * g),
        ):
            if n:
                b = wbuf.at[0, pl.ds(0, n)]
                remote(b, b, ring_send, sem.at[t - 1, g], left).wait_recv()

    @pl.when(first)
    def _():
        pl.semaphore_wait(barrier, len(near))
        pl.when(s == 0)(lambda: v_start(0, CHUNKS, 0))
        clear()
        for sem in range(half + 1):
            blocks = [i for i in range(Z) if (i + 1) // 2 == sem]
            took(len(blocks), sem)
            for i in blocks:
                project(block(order[i]))

    @pl.when(second)
    def _():
        wb_copy.wait()
        wbuf[z, x, yl, 128:144, :] = jnp.broadcast_to(wb[...], (16, 128))
        w_copy.wait()

        @pl.when(s == 1)
        def _():
            pl.semaphore_wait(barrier, len(near))
            v_start(0, EARLY, 1)
            pl.semaphore_wait(go, 1)

        @pl.when(s == 3)
        def _():
            pl.semaphore_wait(barrier, len(near) + len(far))
            y_copies[0].start()
            for peer in far:
                pl.semaphore_signal(ready, inc=1, device_id=peer, device_id_type=MESH)
            pl.semaphore_wait(ready, len(far))
            pl.semaphore_signal(go, inc=1, device_id=cross, device_id_type=MESH)
            y_copies[1].start()

        y_copies[0].wait_recv()
        for c in x_copies:
            c.start()
        ring(1, 0)
        clear()
        b = wbuf.at[0, pl.ds(0, X - 1)]
        remote(b, b, x_send, x_recv, sib).wait_recv()
        for j in range(1, X):
            ring(1, j)
        to_sib(0).start()
        project(block(0))
        for t in range(1, half + 1):
            for g in range(2):
                came(t, g)
                if t < half:
                    for j in ((0,), (1, 2, 3))[g]:
                        ring(t + 1, j)
            fresh = [i for i in (2 * t - 1, 2 * t) if i < Z]
            for i in fresh:
                to_sib(i).start()
            for i in fresh:
                project(block(order[i]))

    low = lax.broadcasted_iota(jnp.int32, (tokens, 128), 1) < 64
    low_half = low[: tokens // 2]
    proj = acc[...]
    turned = pltpu.roll(proj, 64, 1)
    logit = dot_t(jnp.ones((8, 128), F32), lacc[...])
    gate = 1.0 / (1.0 + jnp.exp(-logit))
    kown[0:64, :] = jnp.where(low_half, turned[0:64], proj[64:128]).astype(BF16)
    kown[64:80, :] = jnp.concatenate(parts(gate), axis=0)

    def k_copy(src, r, to):
        return remote(src, kbuf.at[r], k_send, k_recv.at[r], to)

    v_sib = remote(values, vbuf.at[s], d_send, d_recv, sib)

    @pl.when(first)
    def _():
        k_copy(kown, s, sib).start()
        v_sib.start()

    @pl.when(s == 1)
    def _():
        k_copy(kown, 1, cross).start()
        k_copy(kown, 0, sib).wait_recv()
        k_copy(kbuf.at[0], 0, cross).start()
        v_start(EARLY, CHUNKS, 1)

    phi_q = phi_of(halves(proj, turned, low))

    def relay(k, c, slot):
        b = vbuf.at[slot, :, c]
        return remote(b, b, r_send, r_recv.at[k], sib)

    def take(k, c, slot):
        v_copy(k, c, slot).wait_recv()
        relay(k, c, slot).start()

    pl.when(s == 2)(lambda: each(0, HALFWAY, lambda k, c, _: take(k, c, 0)))
    pl.when(s == 3)(lambda: each(0, EARLY, lambda k, c, _: take(k, c, 1)))

    @pl.when(s == 2)
    def _():
        for r in (1, 0):
            k_copy(kown, r, sib).wait_recv()

    @pl.when(s == 3)
    def _():
        for r in (1, 0):
            k_copy(kown, r, cross).wait_recv()
            k_copy(kbuf.at[r], r, sib).start()
        k_copy(kown, 2, sib).wait_recv()

    @pl.when(s > 0)
    def _():
        keeps, phis, betas, gains = [], [], [], []
        norm = jnp.zeros((1, 128 * NU), F32)
        for r in range(SEGS - 1):
            two = kbuf[r, 0:64, :].astype(F32)
            two_turned = pltpu.roll(two, 64, 1)
            p = jnp.concatenate(
                [halves(two, two_turned, low_half), halves(two_turned, two, low_half)], axis=0
            )
            phi = phi_of(p)
            gates = kbuf[r, 64:80, :].astype(F32)
            beta = gates[0:8] + gates[8:16]
            if r:
                div = jnp.maximum(dot_t(jnp.broadcast_to(norm, (8, 128 * NU)), phi), 1.0)
            keep = jnp.where((idm[0, r + 1] == idm[0, r]) | (s < r + 1), 1.0, 0.0).astype(F32)
            phis.append(phi)
            betas.append(beta[0:1])
            gains.append((beta / div)[0:1] if r else None)
            keeps.append(keep)
            norm = keep * (norm + jnp.sum(phi, axis=0, keepdims=True))
        scale = 1.0 / jnp.maximum(jnp.sum(phi_q * norm, axis=1, keepdims=True), 1.0)
        q = phi_q
        for r in reversed(range(SEGS - 1)):
            q = keeps[r] * q
            t = dot_t(q, phis[r])
            m = t * betas[r] * scale
            mats[:, 128 * r : 128 * (r + 1)] = m.astype(BF16)
            if r:
                q = q - dot(t * gains[r], phis[r])

    def mix_step(c, wide, n):
        v = vbuf[0:n, :, c].reshape(128 * n, wide)
        out[:, c] = jnp.dot(mats[:, : 128 * n], v, preferred_element_type=F32).astype(BF16)

    def mix(c, wide, n):
        if wide <= STEP:
            mix_step(c, wide, n)
        else:

            @pl.loop(0, wide // STEP)
            def _(i):
                mix_step(pl.ds(pl.multiple_of(c.start + i * STEP, 256), STEP), STEP, n)

    @pl.when(s == 0)
    def _():
        out[...] = jnp.zeros_like(out)

    @pl.when(s == 1)
    def _():
        remote(values, vbuf.at[0], d_send, d_recv, sib).wait_recv()
        each(0, CHUNKS, lambda k, c, wide: mix(c, wide, 1))

    def use(k, c, wide, slot, n):
        relay(k, c, 1 - slot).wait_recv()
        mix(c, wide, n)

    @pl.when(s == 2)
    def _():
        each(0, HALFWAY - 1, lambda k, c, wide: use(k, c, wide, 0, 2))

        def body(k, c, wide):
            take(k, c, 0)
            use(k - 1, pl.ds(pl.multiple_of(c.start - wide, 256), wide), wide, 0, 2)

        each(HALFWAY, CHUNKS, body)
        each(CHUNKS - 1, CHUNKS, lambda k, c, wide: use(k, c, wide, 0, 2))
        relay(0, slice(None), 0).wait_send()

    @pl.when(s == 3)
    def _():
        remote(values, vbuf.at[2], d_send, d_recv, sib).wait_recv()

        def body(k, c, wide):
            take(k, c, 1)
            use(k, c, wide, 1, 3)

        each(0, EARLY, lambda k, c, wide: use(k, c, wide, 1, 3))
        each(EARLY, CHUNKS, body)
        relay(0, slice(None), 1).wait_send()

    @pl.when(first)
    def _():
        k_copy(kown, s, sib).wait_send()
        v_sib.wait_send()

    @pl.when(second)
    def _():
        for n, sem in ((Z - 1, ring_send), (Z, s_send)):
            b = wbuf.at[pl.ds(0, n)]
            remote(b, b, sem, s_recv.at[0], sib).wait_send()
        b = wbuf.at[0, pl.ds(0, X - 1)]
        remote(b, b, x_send, x_recv, sib).wait_send()
        b = kbuf.at[pl.ds(0, 2)]
        remote(b, b, k_send, k_recv.at[0], sib).wait_send()

    @pl.when(s == 3)
    def _():
        remote(pair, pair, y_send, y_recv, sib).wait_send()

    @pl.when(s < 2)
    def _():
        remote(values, vbuf.at[0], v_send, v_recv.at[0], cross).wait_send()


def per_device(hidden, value_states, w_in, w_beta, book_ids):
    _, tokens, width = hidden.shape
    dma = pltpu.SemaphoreType.DMA
    hbm = pl.BlockSpec(memory_space=pltpu.HBM)
    mixed = pl.pallas_call(
        kernel,
        out_shape=jax.ShapeDtypeStruct((tokens, width), BF16),
        in_specs=[hbm] * 5,
        out_specs=pl.BlockSpec(memory_space=pltpu.VMEM),
        scratch_shapes=[
            pltpu.VMEM((tokens, width), BF16),
            pltpu.VMEM((Z, X, YL, 144, 128), BF16),
            pltpu.VMEM((SEGS - 1, tokens, width), BF16),
            pltpu.VMEM((80, 128), BF16),
            pltpu.VMEM((SEGS - 1, 80, 128), BF16),
            pltpu.VMEM((tokens, 128 * (SEGS - 1)), BF16),
            pltpu.VMEM((tokens, 128), F32),
            pltpu.VMEM((tokens, 128), F32),
            pltpu.VMEM((1, 128), BF16), pltpu.SMEM((1, SEGS), jnp.int32),
            pltpu.SemaphoreType.REGULAR, pltpu.SemaphoreType.REGULAR,
            dma, dma, dma, dma, dma, dma, dma, dma, dma, dma((Z // 2, 2)), dma((Z // 2, 2)),
            dma, dma((Z // 2 + 1,)), dma, dma((SEGS - 1,)),
            dma, dma((CHUNKS,)), dma, dma((CHUNKS,)), dma, dma,
        ],
        compiler_params=pltpu.CompilerParams(
            collective_id=0, has_side_effects=True, vmem_limit_bytes=32 << 20
        ),
    )(*(
        pltpu.with_memory_space_constraint(a, pltpu.HBM)
        for a in (hidden[0], value_states[0], w_in, w_beta.reshape(1, 128), book_ids)
    ))
    return mixed[None]


def solution(mesh):
    return jax.shard_map(
        per_device,
        mesh=mesh,
        in_specs=(
            P("fsdp", "seg", None),
            P("fsdp", "seg", None),
            P("fsdp", None),
            P("fsdp"),
            P("fsdp", None),
        ),
        out_specs=P("fsdp", "seg", None),
        check_vma=False,
    )
```

```python
import functools

import jax
import jax.numpy as jnp
from jax import lax
from jax.experimental import pallas as pl
from jax.experimental.pallas import tpu as pltpu
from jax.sharding import PartitionSpec as P

NU = 3
X, Z, YL, SEGS = 4, 8, 2, 4
X_ORDER = (1, 3, 2)
GROUPS = ((0, 1, 4096), (1, 8, 512))
CHUNKS = 9
EARLY = 2
HALFWAY = 2
STEP = 512
MESH = pl.DeviceIdType.MESH
F32, BF16 = jnp.float32, jnp.bfloat16


def parts(a):
    high = a.astype(BF16)
    return high, (a - high.astype(F32)).astype(BF16)


def dot(a, b, dims=(((1,), (0,)), ((), ()))):
    (a_hi, a_lo), (b_hi, b_lo) = parts(a), parts(b)

    def one(x, y):
        return lax.dot_general(x, y, dims, preferred_element_type=F32)

    return one(a_hi, b_hi) + (one(a_hi, b_lo) + one(a_lo, b_hi))


def dot_t(a, b):
    return dot(a, b, (((1,), (1,)), ((), ())))


def halves(u, turned, low):
    return jnp.where(low, jnp.maximum(u, 0.0), jnp.maximum(-turned, 0.0))


def phi_of(p):
    return jnp.concatenate([p * pltpu.roll(p, j, 1) for j in range(1, NU + 1)], axis=1)


def kernel(
    hidden, values, w_in, w_beta, ids, out,
    hid, wbuf, vbuf, kown, kbuf, mats, acc, lacc,
    wb, idm, ready, go, hid_sem, w_sem, wb_sem, id_sem, y_send, y_recv, x_send, x_recv, ring_send, ring_recv,
    s_send, s_recv, k_send, k_recv, v_send, v_recv, r_send, r_recv, d_send, d_recv,
):
    s, f = lax.axis_index("seg"), lax.axis_index("fsdp")
    core, yl = lax.rem(s, 2), lax.rem(f, YL)
    z = lax.rem(lax.div(f, YL), Z)
    x = lax.div(f, YL * Z)
    tokens = hid.shape[0]
    first, second = core == 0, core == 1

    def at(x_, z_, yl_):
        return (x_ * Z + z_) * YL + yl_

    sib = (s + 1 - 2 * core, f)
    cross = (lax.rem(s + 2, SEGS), f)
    y_peer = (s, at(x, z, 1 - yl))
    y_cross = (lax.rem(s + 2, SEGS), at(x, z, 1 - yl))
    x_peer = [(s, at(lax.rem(x + d, X), z, yl)) for d in X_ORDER]
    right = (s, at(x, lax.rem(z + 1, Z), yl))
    left = (s, at(x, lax.rem(z + Z - 1, Z), yl))

    def remote(src, dst, send, recv, to):
        return pltpu.make_async_remote_copy(
            src_ref=src, dst_ref=dst, send_sem=send, recv_sem=recv, device_id=to, device_id_type=MESH
        )

    barrier = pltpu.get_barrier_semaphore()
    near, far = [cross, sib], [y_peer, *x_peer, right, left]

    def greet(peers):
        for peer in peers:
            pl.semaphore_signal(barrier, inc=1, device_id=peer, device_id_type=MESH)

    greet(near)
    pl.when(s == 3)(lambda: greet(far))
    hid_copy = pltpu.make_async_copy(hidden, hid, hid_sem)
    w_copy = pltpu.make_async_copy(w_in, wbuf.at[z, x, yl, pl.ds(0, 128)], w_sem)
    wb_copy = pltpu.make_async_copy(w_beta, wb, wb_sem)
    id_copy = pltpu.make_async_copy(ids, idm, id_sem)

    @pl.when(second)
    def _():
        w_copy.start()
        wb_copy.start()

    hid_copy.start()
    id_copy.start()
    for r in range(SEGS - 1):

        @pl.when(s <= r)
        def _(r=r):
            kbuf[r] = jnp.zeros(kbuf.shape[1:], BF16)

    def each(lo, hi, body):
        for start, count, wide in GROUPS:
            col0 = sum(min(max(start - a, 0), n) * w for a, n, w in GROUPS)
            a, b = max(lo, start), min(hi, start + count)
            if a < b:

                @pl.loop(a, b)
                def _(k):
                    body(k, pl.ds(pl.multiple_of(col0 + (k - start) * wide, 256), wide), wide)

    def v_copy(k, c, slot):
        return remote(values.at[:, c], vbuf.at[slot, :, c], v_send, v_recv.at[k], cross)

    def v_start(lo, hi, slot):
        each(lo, hi, lambda k, c, _: v_copy(k, c, slot).start())

    def project(zb):
        total = jnp.zeros((tokens, 128), F32)
        gate = jnp.zeros((tokens, 128), F32)
        for xb in range(X):
            lo = pl.multiple_of(at(xb, zb, 0) * 128, 128 * YL)
            h = hid[:, pl.ds(lo, 128 * YL)]
            w = jnp.concatenate([wbuf[zb, xb, p, 0:128, :] for p in range(YL)], axis=0)
            total += jnp.dot(h, w, preferred_element_type=F32)
            for p in range(YL):
                row = wbuf[zb, xb, p, 128:144, :][0:1].astype(F32)
                gate += h[:, 128 * p : 128 * (p + 1)].astype(F32) * row
        acc[...] += total
        lacc[...] += gate

    def block(d):
        return lax.rem(z + d + Z, Z)

    half = Z // 2
    order = [0] + [d for t in range(1, half) for d in (-t, t)] + [half]

    def to_sib(i):
        b = wbuf.at[block(order[i])]
        return remote(b, b, s_send, s_recv.at[(i + 1) // 2], sib)

    def took(n, sem):
        b = wbuf.at[pl.ds(0, n)]
        remote(b, b, s_send, s_recv.at[sem], sib).wait_recv()

    def clear():
        acc[...] = jnp.zeros_like(acc)
        lacc[...] = jnp.zeros_like(lacc)
        hid_copy.wait()
        id_copy.wait()

    own, pair = wbuf.at[z, x, yl], wbuf.at[z, x]
    y_copies = [remote(own, own, y_send, y_recv, to) for to in (y_peer, y_cross)]
    x_copies = [remote(pair, pair, x_send, x_recv, peer) for peer in x_peer]

    def ring(t, j):
        xs, g = lax.rem(x + X - (0, *X_ORDER)[j], X), min(j, 1)
        if t < half or j < X // 2:
            b = wbuf.at[block(1 - t), xs]
            remote(b, b, ring_send, ring_recv.at[t - 1, g], right).start()
        if t < half or j >= X // 2:
            b = wbuf.at[block(t - 1), xs]
            remote(b, b, ring_send, ring_recv.at[t - 1, g], left).start()

    def came(t, g):
        if t < half:
            b = wbuf.at[pl.ds(0, 2), pl.ds(0, (1, 3)[g])]
        else:
            b = wbuf.at[0, pl.ds(0, (1, 3)[g])]
        remote(b, b, ring_send, ring_recv.at[t - 1, g], left).wait_recv()

    @pl.when(first)
    def _():
        pl.semaphore_wait(barrier, len(near))
        pl.when(s == 0)(lambda: v_start(0, CHUNKS, 0))
        clear()
        for sem in range(half + 1):
            blocks = [i for i in range(Z) if (i + 1) // 2 == sem]
            took(len(blocks), sem)
            for i in blocks:
                project(block(order[i]))

    @pl.when(second)
    def _():
        wb_copy.wait()
        wbuf[z, x, yl, 128:144, :] = jnp.broadcast_to(wb[...], (16, 128))
        w_copy.wait()

        @pl.when(s == 1)
        def _():
            pl.semaphore_wait(barrier, len(near))
            v_start(0, EARLY, 1)
            pl.semaphore_wait(go, 1)

        @pl.when(s == 3)
        def _():
            pl.semaphore_wait(barrier, len(near) + len(far))
            y_copies[0].start()
            for peer in far:
                pl.semaphore_signal(ready, inc=1, device_id=peer, device_id_type=MESH)
            pl.semaphore_wait(ready, len(far))
            pl.semaphore_signal(go, inc=1, device_id=cross, device_id_type=MESH)
            y_copies[1].start()

        y_copies[0].wait_recv()
        for c in x_copies:
            c.start()
        ring(1, 0)
        clear()
        b = wbuf.at[0, pl.ds(0, X - 1)]
        remote(b, b, x_send, x_recv, sib).wait_recv()
        for j in range(1, X):
            ring(1, j)
        to_sib(0).start()
        project(block(0))
        for t in range(1, half + 1):
            for g in range(2):
                came(t, g)
                if t < half:
                    for j in ((0,), (1, 2, 3))[g]:
                        ring(t + 1, j)
            fresh = [i for i in (2 * t - 1, 2 * t) if i < Z]
            for i in fresh:
                to_sib(i).start()
            for i in fresh:
                project(block(order[i]))

    low = lax.broadcasted_iota(jnp.int32, (tokens, 128), 1) < 64
    low_half = low[: tokens // 2]
    proj = acc[...]
    turned = pltpu.roll(proj, 64, 1)
    logit = dot_t(jnp.ones((8, 128), F32), lacc[...])
    gate = 1.0 / (1.0 + jnp.exp(-logit))
    kown[1, 0:64, :] = jnp.where(low_half, turned[0:64], proj[64:128]).astype(BF16)
    kown[1, 64:80, :] = jnp.concatenate(parts(gate), axis=0)

    def k_copy(src, lo, n, to):
        return remote(src, kbuf.at[pl.ds(lo, n)], k_send, k_recv.at[lo // 2], to)

    k_own = kown.at[pl.ds(1, 1)]
    v_sib = remote(values, vbuf.at[s], d_send, d_recv, sib)

    @pl.when(first)
    def _():
        remote(k_own, kbuf.at[pl.ds(s, 1)], k_send, k_recv.at[lax.div(s, 2)], sib).start()
        v_sib.start()

    @pl.when(s == 1)
    def _():
        k_copy(k_own, 0, 1, sib).wait_recv()
        kown[0] = kbuf[0]
        k_copy(kown, 0, 2, cross).start()
        v_start(EARLY, CHUNKS, 1)

    phi_q = phi_of(halves(proj, turned, low))

    def relay(k, c, slot):
        b = vbuf.at[slot, :, c]
        return remote(b, b, r_send, r_recv.at[k], sib)

    def take(k, c, slot):
        v_copy(k, c, slot).wait_recv()
        relay(k, c, slot).start()

    pl.when(s == 2)(lambda: each(0, HALFWAY, lambda k, c, _: take(k, c, 0)))
    pl.when(s == 3)(lambda: each(0, EARLY, lambda k, c, _: take(k, c, 1)))

    k_two = kbuf.at[pl.ds(0, 2)]

    @pl.when(s == 2)
    def _():
        k_copy(k_two, 0, 2, sib).wait_recv()

    @pl.when(s == 3)
    def _():
        k_copy(k_two, 0, 2, cross).wait_recv()
        k_copy(k_two, 0, 2, sib).start()
        k_copy(k_own, 2, 1, sib).wait_recv()

    @pl.when(s > 0)
    def _():
        keeps, phis, betas, gains = [], [], [], []
        norm = jnp.zeros((1, 128 * NU), F32)
        for r in range(SEGS - 1):
            two = kbuf[r, 0:64, :].astype(F32)
            two_turned = pltpu.roll(two, 64, 1)
            p = jnp.concatenate(
                [halves(two, two_turned, low_half), halves(two_turned, two, low_half)], axis=0
            )
            phi = phi_of(p)
            gates = kbuf[r, 64:80, :].astype(F32)
            beta = gates[0:8] + gates[8:16]
            if r:
                div = jnp.maximum(dot_t(jnp.broadcast_to(norm, (8, 128 * NU)), phi), 1.0)
            keep = jnp.where((idm[0, r + 1] == idm[0, r]) | (s < r + 1), 1.0, 0.0).astype(F32)
            phis.append(phi)
            betas.append(beta[0:1])
            gains.append((beta / div)[0:1] if r else None)
            keeps.append(keep)
            norm = keep * (norm + jnp.sum(phi, axis=0, keepdims=True))
        scale = 1.0 / jnp.maximum(jnp.sum(phi_q * norm, axis=1, keepdims=True), 1.0)
        q = phi_q
        for r in reversed(range(SEGS - 1)):
            q = keeps[r] * q
            t = dot_t(q, phis[r])
            m = t * betas[r] * scale
            mats[:, 128 * r : 128 * (r + 1)] = m.astype(BF16)
            if r:
                q = q - dot(t * gains[r], phis[r])

    def mix_step(c, wide, n):
        v = vbuf[0:n, :, c].reshape(128 * n, wide)
        out[:, c] = jnp.dot(mats[:, : 128 * n], v, preferred_element_type=F32).astype(BF16)

    def mix(c, wide, n):
        if wide <= STEP:
            mix_step(c, wide, n)
        else:

            @pl.loop(0, wide // STEP)
            def _(i):
                mix_step(pl.ds(pl.multiple_of(c.start + i * STEP, 256), STEP), STEP, n)

    @pl.when(s == 0)
    def _():
        out[...] = jnp.zeros_like(out)

    @pl.when(s == 1)
    def _():
        remote(values, vbuf.at[0], d_send, d_recv, sib).wait_recv()
        each(0, CHUNKS, lambda k, c, wide: mix(c, wide, 1))

    def use(k, c, wide, slot, n):
        relay(k, c, 1 - slot).wait_recv()
        mix(c, wide, n)

    @pl.when(s == 2)
    def _():
        each(0, HALFWAY - 1, lambda k, c, wide: use(k, c, wide, 0, 2))

        def body(k, c, wide):
            take(k, c, 0)
            use(k - 1, pl.ds(pl.multiple_of(c.start - wide, 256), wide), wide, 0, 2)

        each(HALFWAY, CHUNKS, body)
        each(CHUNKS - 1, CHUNKS, lambda k, c, wide: use(k, c, wide, 0, 2))
        relay(0, slice(None), 0).wait_send()

    @pl.when(s == 3)
    def _():
        remote(values, vbuf.at[2], d_send, d_recv, sib).wait_recv()

        def body(k, c, wide):
            take(k, c, 1)
            use(k, c, wide, 1, 3)

        each(0, EARLY, lambda k, c, wide: use(k, c, wide, 1, 3))
        each(EARLY, CHUNKS, body)
        relay(0, slice(None), 1).wait_send()

    @pl.when(first)
    def _():
        k_copy(k_own, 0, 1, sib).wait_send()
        v_sib.wait_send()

    @pl.when(second)
    def _():
        for n, sem in ((Z - 1, ring_send), (Z, s_send)):
            b = wbuf.at[pl.ds(0, n)]
            remote(b, b, sem, s_recv.at[0], sib).wait_send()
        b = wbuf.at[0, pl.ds(0, X - 1)]
        remote(b, b, x_send, x_recv, sib).wait_send()
        k_copy(k_two, 0, 2, sib).wait_send()

    @pl.when(s == 3)
    def _():
        remote(pair, pair, y_send, y_recv, sib).wait_send()

    @pl.when(s < 2)
    def _():
        remote(values, vbuf.at[0], v_send, v_recv.at[0], cross).wait_send()


def per_device(hidden, value_states, w_in, w_beta, book_ids):
    _, tokens, width = hidden.shape
    dma = pltpu.SemaphoreType.DMA
    hbm = pl.BlockSpec(memory_space=pltpu.HBM)
    mixed = pl.pallas_call(
        kernel,
        out_shape=jax.ShapeDtypeStruct((tokens, width), BF16),
        in_specs=[hbm] * 5,
        out_specs=pl.BlockSpec(memory_space=pltpu.VMEM),
        scratch_shapes=[
            pltpu.VMEM((tokens, width), BF16),
            pltpu.VMEM((Z, X, YL, 144, 128), BF16),
            pltpu.VMEM((SEGS - 1, tokens, width), BF16),
            pltpu.VMEM((2, 80, 128), BF16),
            pltpu.VMEM((SEGS - 1, 80, 128), BF16),
            pltpu.VMEM((tokens, 128 * (SEGS - 1)), BF16),
            pltpu.VMEM((tokens, 128), F32),
            pltpu.VMEM((tokens, 128), F32),
            pltpu.VMEM((1, 128), BF16), pltpu.SMEM((1, SEGS), jnp.int32),
            pltpu.SemaphoreType.REGULAR, pltpu.SemaphoreType.REGULAR,
            dma, dma, dma, dma, dma, dma, dma, dma, dma, dma((Z // 2, 2)),
            dma, dma((Z // 2 + 1,)), dma, dma((2,)),
            dma, dma((CHUNKS,)), dma, dma((CHUNKS,)), dma, dma,
        ],
        compiler_params=pltpu.CompilerParams(
            collective_id=0, has_side_effects=True, vmem_limit_bytes=32 << 20
        ),
    )(*(
        pltpu.with_memory_space_constraint(a, pltpu.HBM)
        for a in (hidden[0], value_states[0], w_in, w_beta.reshape(1, 128), book_ids)
    ))
    return mixed[None]


def solution(mesh):
    return jax.shard_map(
        per_device,
        mesh=mesh,
        in_specs=(
            P("fsdp", "seg", None),
            P("fsdp", "seg", None),
            P("fsdp", None),
            P("fsdp"),
            P("fsdp", None),
        ),
        out_specs=P("fsdp", "seg", None),
        check_vma=False,
    )
```

```python
import functools

import jax
import jax.numpy as jnp
from jax import lax
from jax.experimental import pallas as pl
from jax.experimental.pallas import tpu as pltpu
from jax.sharding import PartitionSpec as P

NU = 3
X, Z, YL, SEGS = 4, 8, 2, 4
X_ORDER = (1, 3, 2)
GROUPS = ((0, 1, 4096), (1, 8, 512))
CHUNKS = 9
EARLY = 2
HALFWAY = 2
STEP = 512
MESH = pl.DeviceIdType.MESH
F32, BF16 = jnp.float32, jnp.bfloat16


def parts(a):
    high = a.astype(BF16)
    return high, (a - high.astype(F32)).astype(BF16)


def dot(a, b, dims=(((1,), (0,)), ((), ()))):
    (a_hi, a_lo), (b_hi, b_lo) = parts(a), parts(b)

    def one(x, y):
        return lax.dot_general(x, y, dims, preferred_element_type=F32)

    return one(a_hi, b_hi) + (one(a_hi, b_lo) + one(a_lo, b_hi))


def dot_t(a, b):
    return dot(a, b, (((1,), (1,)), ((), ())))


def halves(u, turned, low):
    return jnp.where(low, jnp.maximum(u, 0.0), jnp.maximum(-turned, 0.0))


def phi_of(p):
    return jnp.concatenate([p * pltpu.roll(p, j, 1) for j in range(1, NU + 1)], axis=1)


def kernel(
    hidden, values, w_in, w_beta, ids, out,
    hid, wbuf, vbuf, kown, kbuf, mats, acc, lacc,
    wb, idm, ready, go, hid_sem, w_sem, wb_sem, id_sem, y_send, y_recv, x_send, x_recv, ring_send, ring_recv,
    s_send, s_recv, k_send, k_recv, v_send, v_recv, r_send, r_recv, d_send, d_recv,
):
    s, f = lax.axis_index("seg"), lax.axis_index("fsdp")
    core, yl = lax.rem(s, 2), lax.rem(f, YL)
    z = lax.rem(lax.div(f, YL), Z)
    x = lax.div(f, YL * Z)
    tokens = hid.shape[0]
    first, second = core == 0, core == 1

    def at(x_, z_, yl_):
        return (x_ * Z + z_) * YL + yl_

    sib = (s + 1 - 2 * core, f)
    cross = (lax.rem(s + 2, SEGS), f)
    y_peer = (s, at(x, z, 1 - yl))
    y_cross = (lax.rem(s + 2, SEGS), at(x, z, 1 - yl))
    x_peer = [(s, at(lax.rem(x + d, X), z, yl)) for d in X_ORDER]
    right = (s, at(x, lax.rem(z + 1, Z), yl))
    left = (s, at(x, lax.rem(z + Z - 1, Z), yl))

    def remote(src, dst, send, recv, to):
        return pltpu.make_async_remote_copy(
            src_ref=src, dst_ref=dst, send_sem=send, recv_sem=recv, device_id=to, device_id_type=MESH
        )

    barrier = pltpu.get_barrier_semaphore()
    near, far = [cross, sib], [y_peer, *x_peer, right, left]

    def greet(peers):
        for peer in peers:
            pl.semaphore_signal(barrier, inc=1, device_id=peer, device_id_type=MESH)

    greet(near)
    pl.when(s == 3)(lambda: greet(far))
    hid_copy = pltpu.make_async_copy(hidden, hid, hid_sem)
    w_copy = pltpu.make_async_copy(w_in, wbuf.at[z, x, yl, pl.ds(0, 128)], w_sem)
    wb_copy = pltpu.make_async_copy(w_beta, wb, wb_sem)
    id_copy = pltpu.make_async_copy(ids, idm, id_sem)

    @pl.when(second)
    def _():
        w_copy.start()
        wb_copy.start()

    hid_copy.start()
    id_copy.start()
    for r in range(SEGS - 1):

        @pl.when(s <= r)
        def _(r=r):
            kbuf[r] = jnp.zeros(kbuf.shape[1:], BF16)

    def each(lo, hi, body):
        for start, count, wide in GROUPS:
            col0 = sum(min(max(start - a, 0), n) * w for a, n, w in GROUPS)
            a, b = max(lo, start), min(hi, start + count)
            if a < b:

                @pl.loop(a, b)
                def _(k):
                    body(k, pl.ds(pl.multiple_of(col0 + (k - start) * wide, 256), wide), wide)

    def v_copy(k, c, slot):
        return remote(values.at[:, c], vbuf.at[slot, :, c], v_send, v_recv.at[k], cross)

    def v_start(lo, hi, slot):
        each(lo, hi, lambda k, c, _: v_copy(k, c, slot).start())

    def project(zb):
        total = jnp.zeros((tokens, 128), F32)
        gate = jnp.zeros((tokens, 128), F32)
        for xb in range(X):
            lo = pl.multiple_of(at(xb, zb, 0) * 128, 128 * YL)
            h = hid[:, pl.ds(lo, 128 * YL)]
            w = jnp.concatenate([wbuf[zb, xb, p, 0:128, :] for p in range(YL)], axis=0)
            total += jnp.dot(h, w, preferred_element_type=F32)
            for p in range(YL):
                row = wbuf[zb, xb, p, 128:144, :][0:1].astype(F32)
                gate += h[:, 128 * p : 128 * (p + 1)].astype(F32) * row
        acc[...] += total
        lacc[...] += gate

    def block(d):
        return lax.rem(z + d + Z, Z)

    half = Z // 2
    order = [0] + [d for t in range(1, half) for d in (-t, t)] + [half]

    def to_sib(i):
        b = wbuf.at[block(order[i])]
        return remote(b, b, s_send, s_recv.at[(i + 1) // 2], sib)

    def took(n, sem):
        b = wbuf.at[pl.ds(0, n)]
        remote(b, b, s_send, s_recv.at[sem], sib).wait_recv()

    def clear():
        acc[...] = jnp.zeros_like(acc)
        lacc[...] = jnp.zeros_like(lacc)
        hid_copy.wait()
        id_copy.wait()

    own, pair = wbuf.at[z, x, yl], wbuf.at[z, x]
    y_copies = [remote(own, own, y_send, y_recv, to) for to in (y_peer, y_cross)]
    x_copies = [remote(pair, pair, x_send, x_recv, peer) for peer in x_peer]

    def ring(t, j):
        xs, g = lax.rem(x + X - (0, *X_ORDER)[j], X), min(j, 1)
        if t < half or j < X // 2:
            b = wbuf.at[block(1 - t), xs]
            remote(b, b, ring_send, ring_recv.at[t - 1, g], right).start()
        if t < half or j >= X // 2:
            b = wbuf.at[block(t - 1), xs]
            remote(b, b, ring_send, ring_recv.at[t - 1, g], left).start()

    def came(t, g):
        if t < half:
            b = wbuf.at[pl.ds(0, 2), pl.ds(0, (1, 3)[g])]
        else:
            b = wbuf.at[0, pl.ds(0, (1, 3)[g])]
        remote(b, b, ring_send, ring_recv.at[t - 1, g], left).wait_recv()

    @pl.when(first)
    def _():
        pl.semaphore_wait(barrier, len(near))
        pl.when(s == 0)(lambda: v_start(0, CHUNKS, 0))
        clear()
        for sem in range(half + 1):
            blocks = [i for i in range(Z) if (i + 1) // 2 == sem]
            took(len(blocks), sem)
            for i in blocks:
                project(block(order[i]))

    @pl.when(second)
    def _():
        @pl.when(s == 1)
        def _():
            pl.semaphore_wait(barrier, len(near))
            v_start(0, EARLY, 1)


        wb_copy.wait()
        wbuf[z, x, yl, 128:144, :] = jnp.broadcast_to(wb[...], (16, 128))
        w_copy.wait()

        pl.when(s == 1)(lambda: pl.semaphore_wait(go, 1))

        @pl.when(s == 3)
        def _():
            pl.semaphore_wait(barrier, len(near) + len(far))
            y_copies[0].start()
            for peer in far:
                pl.semaphore_signal(ready, inc=1, device_id=peer, device_id_type=MESH)
            pl.semaphore_wait(ready, len(far))
            pl.semaphore_signal(go, inc=1, device_id=cross, device_id_type=MESH)
            y_copies[1].start()

        y_copies[0].wait_recv()
        for c in x_copies:
            c.start()
        ring(1, 0)
        clear()
        b = wbuf.at[0, pl.ds(0, X - 1)]
        remote(b, b, x_send, x_recv, sib).wait_recv()
        for j in range(1, X):
            ring(1, j)
        to_sib(0).start()
        project(block(0))
        for t in range(1, half + 1):
            for g in range(2):
                came(t, g)
                if t < half:
                    for j in ((0,), (1, 2, 3))[g]:
                        ring(t + 1, j)
            fresh = [i for i in (2 * t - 1, 2 * t) if i < Z]
            for i in fresh:
                to_sib(i).start()
            for i in fresh:
                project(block(order[i]))

    low = lax.broadcasted_iota(jnp.int32, (tokens, 128), 1) < 64
    low_half = low[: tokens // 2]
    proj = acc[...]
    turned = pltpu.roll(proj, 64, 1)
    logit = dot_t(jnp.ones((8, 128), F32), lacc[...])
    gate = 1.0 / (1.0 + jnp.exp(-logit))
    kown[1, 0:64, :] = jnp.where(low_half, turned[0:64], proj[64:128]).astype(BF16)
    kown[1, 64:80, :] = jnp.concatenate(parts(gate), axis=0)

    def k_copy(src, lo, n, to):
        return remote(src, kbuf.at[pl.ds(lo, n)], k_send, k_recv.at[lo // 2], to)

    k_own = kown.at[pl.ds(1, 1)]
    v_sib = remote(values, vbuf.at[s], d_send, d_recv, sib)

    @pl.when(first)
    def _():
        remote(k_own, kbuf.at[pl.ds(s, 1)], k_send, k_recv.at[lax.div(s, 2)], sib).start()
        v_sib.start()

    @pl.when(s == 1)
    def _():
        k_copy(k_own, 0, 1, sib).wait_recv()
        kown[0] = kbuf[0]
        k_copy(kown, 0, 2, cross).start()
        v_start(EARLY, CHUNKS, 1)

    phi_q = phi_of(halves(proj, turned, low))

    def relay(k, c, slot):
        b = vbuf.at[slot, :, c]
        return remote(b, b, r_send, r_recv.at[k], sib)

    def take(k, c, slot):
        v_copy(k, c, slot).wait_recv()
        relay(k, c, slot).start()

    pl.when(s == 2)(lambda: each(0, HALFWAY, lambda k, c, _: take(k, c, 0)))
    pl.when(s == 3)(lambda: each(0, EARLY, lambda k, c, _: take(k, c, 1)))

    k_two = kbuf.at[pl.ds(0, 2)]

    @pl.when(s == 2)
    def _():
        k_copy(k_two, 0, 2, sib).wait_recv()

    @pl.when(s == 3)
    def _():
        k_copy(k_two, 0, 2, cross).wait_recv()
        k_copy(k_two, 0, 2, sib).start()
        k_copy(k_own, 2, 1, sib).wait_recv()

    @pl.when(s > 0)
    def _():
        keeps, phis, betas, gains = [], [], [], []
        norm = jnp.zeros((1, 128 * NU), F32)
        for r in range(SEGS - 1):
            two = kbuf[r, 0:64, :].astype(F32)
            two_turned = pltpu.roll(two, 64, 1)
            p = jnp.concatenate(
                [halves(two, two_turned, low_half), halves(two_turned, two, low_half)], axis=0
            )
            phi = phi_of(p)
            gates = kbuf[r, 64:80, :].astype(F32)
            beta = gates[0:8] + gates[8:16]
            if r:
                div = jnp.maximum(dot_t(jnp.broadcast_to(norm, (8, 128 * NU)), phi), 1.0)
            keep = jnp.where((idm[0, r + 1] == idm[0, r]) | (s < r + 1), 1.0, 0.0).astype(F32)
            phis.append(phi)
            betas.append(beta[0:1])
            gains.append((beta / div)[0:1] if r else None)
            keeps.append(keep)
            norm = keep * (norm + jnp.sum(phi, axis=0, keepdims=True))
        scale = 1.0 / jnp.maximum(jnp.sum(phi_q * norm, axis=1, keepdims=True), 1.0)
        q = phi_q
        for r in reversed(range(SEGS - 1)):
            q = keeps[r] * q
            t = dot_t(q, phis[r])
            m = t * betas[r] * scale
            mats[:, 128 * r : 128 * (r + 1)] = m.astype(BF16)
            if r:
                q = q - dot(t * gains[r], phis[r])

    def mix_step(c, wide, n):
        v = vbuf[0:n, :, c].reshape(128 * n, wide)
        out[:, c] = jnp.dot(mats[:, : 128 * n], v, preferred_element_type=F32).astype(BF16)

    def mix(c, wide, n):
        if wide <= STEP:
            mix_step(c, wide, n)
        else:

            @pl.loop(0, wide // STEP)
            def _(i):
                mix_step(pl.ds(pl.multiple_of(c.start + i * STEP, 256), STEP), STEP, n)

    @pl.when(s == 0)
    def _():
        out[...] = jnp.zeros_like(out)

    @pl.when(s == 1)
    def _():
        remote(values, vbuf.at[0], d_send, d_recv, sib).wait_recv()
        each(0, CHUNKS, lambda k, c, wide: mix(c, wide, 1))

    def use(k, c, wide, slot, n):
        relay(k, c, 1 - slot).wait_recv()
        mix(c, wide, n)

    @pl.when(s == 2)
    def _():
        each(0, HALFWAY - 1, lambda k, c, wide: use(k, c, wide, 0, 2))

        def body(k, c, wide):
            take(k, c, 0)
            use(k - 1, pl.ds(pl.multiple_of(c.start - wide, 256), wide), wide, 0, 2)

        each(HALFWAY, CHUNKS, body)
        each(CHUNKS - 1, CHUNKS, lambda k, c, wide: use(k, c, wide, 0, 2))
        relay(0, slice(None), 0).wait_send()

    @pl.when(s == 3)
    def _():
        remote(values, vbuf.at[2], d_send, d_recv, sib).wait_recv()

        def body(k, c, wide):
            take(k, c, 1)
            use(k, c, wide, 1, 3)

        each(0, EARLY, lambda k, c, wide: use(k, c, wide, 1, 3))
        each(EARLY, CHUNKS, body)
        relay(0, slice(None), 1).wait_send()

    @pl.when(first)
    def _():
        k_copy(k_own, 0, 1, sib).wait_send()
        v_sib.wait_send()

    @pl.when(second)
    def _():
        for n, sem in ((Z - 1, ring_send), (Z, s_send)):
            b = wbuf.at[pl.ds(0, n)]
            remote(b, b, sem, s_recv.at[0], sib).wait_send()
        b = wbuf.at[0, pl.ds(0, X - 1)]
        remote(b, b, x_send, x_recv, sib).wait_send()
        k_copy(k_two, 0, 2, sib).wait_send()

    @pl.when(s == 3)
    def _():
        remote(pair, pair, y_send, y_recv, sib).wait_send()

    @pl.when(s < 2)
    def _():
        remote(values, vbuf.at[0], v_send, v_recv.at[0], cross).wait_send()


def per_device(hidden, value_states, w_in, w_beta, book_ids):
    _, tokens, width = hidden.shape
    dma = pltpu.SemaphoreType.DMA
    hbm = pl.BlockSpec(memory_space=pltpu.HBM)
    mixed = pl.pallas_call(
        kernel,
        out_shape=jax.ShapeDtypeStruct((tokens, width), BF16),
        in_specs=[hbm] * 5,
        out_specs=pl.BlockSpec(memory_space=pltpu.VMEM),
        scratch_shapes=[
            pltpu.VMEM((tokens, width), BF16),
            pltpu.VMEM((Z, X, YL, 144, 128), BF16),
            pltpu.VMEM((SEGS - 1, tokens, width), BF16),
            pltpu.VMEM((2, 80, 128), BF16),
            pltpu.VMEM((SEGS - 1, 80, 128), BF16),
            pltpu.VMEM((tokens, 128 * (SEGS - 1)), BF16),
            pltpu.VMEM((tokens, 128), F32),
            pltpu.VMEM((tokens, 128), F32),
            pltpu.VMEM((1, 128), BF16), pltpu.SMEM((1, SEGS), jnp.int32),
            pltpu.SemaphoreType.REGULAR, pltpu.SemaphoreType.REGULAR,
            dma, dma, dma, dma, dma, dma, dma, dma, dma, dma((Z // 2, 2)),
            dma, dma((Z // 2 + 1,)), dma, dma((2,)),
            dma, dma((CHUNKS,)), dma, dma((CHUNKS,)), dma, dma,
        ],
        compiler_params=pltpu.CompilerParams(
            collective_id=0, has_side_effects=True, vmem_limit_bytes=32 << 20
        ),
    )(*(
        pltpu.with_memory_space_constraint(a, pltpu.HBM)
        for a in (hidden[0], value_states[0], w_in, w_beta.reshape(1, 128), book_ids)
    ))
    return mixed[None]


def solution(mesh):
    return jax.shard_map(
        per_device,
        mesh=mesh,
        in_specs=(
            P("fsdp", "seg", None),
            P("fsdp", "seg", None),
            P("fsdp", None),
            P("fsdp"),
            P("fsdp", None),
        ),
        out_specs=P("fsdp", "seg", None),
        check_vma=False,
    )
```

```python
import functools

import jax
import jax.numpy as jnp
from jax import lax
from jax.experimental import pallas as pl
from jax.experimental.pallas import tpu as pltpu
from jax.sharding import PartitionSpec as P

NU = 3
X, Z, YL, SEGS = 4, 8, 2, 4
X_ORDER = (1, 3, 2)
GROUPS = ((0, 1, 4608), (1, 7, 512))
CHUNKS = 8
EARLY = 1
HALFWAY = 2
STEP = 512
MESH = pl.DeviceIdType.MESH
F32, BF16 = jnp.float32, jnp.bfloat16


def parts(a):
    high = a.astype(BF16)
    return high, (a - high.astype(F32)).astype(BF16)


def dot(a, b, dims=(((1,), (0,)), ((), ()))):
    (a_hi, a_lo), (b_hi, b_lo) = parts(a), parts(b)

    def one(x, y):
        return lax.dot_general(x, y, dims, preferred_element_type=F32)

    return one(a_hi, b_hi) + (one(a_hi, b_lo) + one(a_lo, b_hi))


def dot_t(a, b):
    return dot(a, b, (((1,), (1,)), ((), ())))


def halves(u, turned, low):
    return jnp.where(low, jnp.maximum(u, 0.0), jnp.maximum(-turned, 0.0))


def phi_of(p):
    return jnp.concatenate([p * pltpu.roll(p, j, 1) for j in range(1, NU + 1)], axis=1)


def kernel(
    hidden, values, w_in, w_beta, ids, out,
    hid, wbuf, vbuf, kown, kbuf, mats, acc, lacc,
    wb, idm, ready, go, hid_sem, w_sem, wb_sem, id_sem, y_send, y_recv, x_send, x_recv, ring_send, ring_recv,
    s_send, s_recv, k_send, k_recv, v_send, v_recv, r_send, r_recv, d_send, d_recv,
):
    s, f = lax.axis_index("seg"), lax.axis_index("fsdp")
    core, yl = lax.rem(s, 2), lax.rem(f, YL)
    z = lax.rem(lax.div(f, YL), Z)
    x = lax.div(f, YL * Z)
    tokens = hid.shape[0]
    first, second = core == 0, core == 1

    def at(x_, z_, yl_):
        return (x_ * Z + z_) * YL + yl_

    sib = (s + 1 - 2 * core, f)
    cross = (lax.rem(s + 2, SEGS), f)
    y_peer = (s, at(x, z, 1 - yl))
    y_cross = (lax.rem(s + 2, SEGS), at(x, z, 1 - yl))
    x_peer = [(s, at(lax.rem(x + d, X), z, yl)) for d in X_ORDER]
    right = (s, at(x, lax.rem(z + 1, Z), yl))
    left = (s, at(x, lax.rem(z + Z - 1, Z), yl))

    def remote(src, dst, send, recv, to):
        return pltpu.make_async_remote_copy(
            src_ref=src, dst_ref=dst, send_sem=send, recv_sem=recv, device_id=to, device_id_type=MESH
        )

    barrier = pltpu.get_barrier_semaphore()
    near, far = [cross, sib], [y_peer, *x_peer, right, left]

    def greet(peers):
        for peer in peers:
            pl.semaphore_signal(barrier, inc=1, device_id=peer, device_id_type=MESH)

    greet(near)
    pl.when(s == 3)(lambda: greet(far))
    hid_copy = pltpu.make_async_copy(hidden, hid, hid_sem)
    w_copy = pltpu.make_async_copy(w_in, wbuf.at[z, x, yl, pl.ds(0, 128)], w_sem)
    wb_copy = pltpu.make_async_copy(w_beta, wb, wb_sem)
    id_copy = pltpu.make_async_copy(ids, idm, id_sem)

    @pl.when(second)
    def _():
        w_copy.start()
        wb_copy.start()

    hid_copy.start()
    id_copy.start()
    for r in range(SEGS - 1):

        @pl.when(s <= r)
        def _(r=r):
            kbuf[r] = jnp.zeros(kbuf.shape[1:], BF16)

    def each(lo, hi, body):
        for start, count, wide in GROUPS:
            col0 = sum(min(max(start - a, 0), n) * w for a, n, w in GROUPS)
            a, b = max(lo, start), min(hi, start + count)
            if a < b:

                @pl.loop(a, b)
                def _(k):
                    body(k, pl.ds(pl.multiple_of(col0 + (k - start) * wide, 256), wide), wide)

    def v_copy(k, c, slot):
        return remote(values.at[:, c], vbuf.at[slot, :, c], v_send, v_recv.at[k], cross)

    def v_start(lo, hi, slot):
        each(lo, hi, lambda k, c, _: v_copy(k, c, slot).start())

    def project(zb):
        total = jnp.zeros((tokens, 128), F32)
        gate = jnp.zeros((tokens, 128), F32)
        for xb in range(X):
            lo = pl.multiple_of(at(xb, zb, 0) * 128, 128 * YL)
            h = hid[:, pl.ds(lo, 128 * YL)]
            w = jnp.concatenate([wbuf[zb, xb, p, 0:128, :] for p in range(YL)], axis=0)
            total += jnp.dot(h, w, preferred_element_type=F32)
            for p in range(YL):
                row = wbuf[zb, xb, p, 128:144, :][0:1].astype(F32)
                gate += h[:, 128 * p : 128 * (p + 1)].astype(F32) * row
        acc[...] += total
        lacc[...] += gate

    def block(d):
        return lax.rem(z + d + Z, Z)

    half = Z // 2
    order = [0] + [d for t in range(1, half) for d in (-t, t)] + [half]

    def to_sib(i):
        b = wbuf.at[block(order[i])]
        return remote(b, b, s_send, s_recv.at[(i + 1) // 2], sib)

    def took(n, sem):
        b = wbuf.at[pl.ds(0, n)]
        remote(b, b, s_send, s_recv.at[sem], sib).wait_recv()

    def clear():
        acc[...] = jnp.zeros_like(acc)
        lacc[...] = jnp.zeros_like(lacc)
        hid_copy.wait()
        id_copy.wait()

    own, pair = wbuf.at[z, x, yl], wbuf.at[z, x]
    y_copies = [remote(own, own, y_send, y_recv, to) for to in (y_peer, y_cross)]
    x_copies = [remote(pair, pair, x_send, x_recv, peer) for peer in x_peer]

    def ring(t, j):
        xs, g = lax.rem(x + X - (0, *X_ORDER)[j], X), min(j, 1)
        if t < half or j < X // 2:
            b = wbuf.at[block(1 - t), xs]
            remote(b, b, ring_send, ring_recv.at[t - 1, g], right).start()
        if t < half or j >= X // 2:
            b = wbuf.at[block(t - 1), xs]
            remote(b, b, ring_send, ring_recv.at[t - 1, g], left).start()

    def came(t, g):
        if t < half:
            b = wbuf.at[pl.ds(0, 2), pl.ds(0, (1, 3)[g])]
        else:
            b = wbuf.at[0, pl.ds(0, (1, 3)[g])]
        remote(b, b, ring_send, ring_recv.at[t - 1, g], left).wait_recv()

    @pl.when(first)
    def _():
        pl.semaphore_wait(barrier, len(near))
        pl.when(s == 0)(lambda: v_start(0, CHUNKS, 0))
        clear()
        for sem in range(half + 1):
            blocks = [i for i in range(Z) if (i + 1) // 2 == sem]
            took(len(blocks), sem)
            for i in blocks:
                project(block(order[i]))

    @pl.when(second)
    def _():
        wb_copy.wait()
        wbuf[z, x, yl, 128:144, :] = jnp.broadcast_to(wb[...], (16, 128))
        w_copy.wait()

        @pl.when(s == 1)
        def _():
            pl.semaphore_wait(barrier, len(near))
            v_start(0, EARLY, 1)
            pl.semaphore_wait(go, 1)

        @pl.when(s == 3)
        def _():
            pl.semaphore_wait(barrier, len(near) + len(far))
            y_copies[0].start()
            for peer in far:
                pl.semaphore_signal(ready, inc=1, device_id=peer, device_id_type=MESH)
            pl.semaphore_wait(ready, len(far))
            pl.semaphore_signal(go, inc=1, device_id=cross, device_id_type=MESH)
            y_copies[1].start()

        y_copies[0].wait_recv()
        for c in x_copies:
            c.start()
        ring(1, 0)
        clear()
        b = wbuf.at[0, pl.ds(0, X - 1)]
        remote(b, b, x_send, x_recv, sib).wait_recv()
        for j in range(1, X):
            ring(1, j)
        to_sib(0).start()
        project(block(0))
        for t in range(1, half + 1):
            for g in range(2):
                came(t, g)
                if t < half:
                    for j in ((0,), (1, 2, 3))[g]:
                        ring(t + 1, j)
            fresh = [i for i in (2 * t - 1, 2 * t) if i < Z]
            for i in fresh:
                to_sib(i).start()
            for i in fresh:
                project(block(order[i]))

    low = lax.broadcasted_iota(jnp.int32, (tokens, 128), 1) < 64
    low_half = low[: tokens // 2]
    proj = acc[...]
    turned = pltpu.roll(proj, 64, 1)
    logit = dot_t(jnp.ones((8, 128), F32), lacc[...])
    gate = 1.0 / (1.0 + jnp.exp(-logit))
    kown[1, 0:64, :] = jnp.where(low_half, turned[0:64], proj[64:128]).astype(BF16)
    kown[1, 64:80, :] = jnp.concatenate(parts(gate), axis=0)

    def k_copy(src, lo, n, to):
        return remote(src, kbuf.at[pl.ds(lo, n)], k_send, k_recv.at[lo // 2], to)

    k_own = kown.at[pl.ds(1, 1)]
    v_sib = remote(values, vbuf.at[s], d_send, d_recv, sib)

    @pl.when(first)
    def _():
        remote(k_own, kbuf.at[pl.ds(s, 1)], k_send, k_recv.at[lax.div(s, 2)], sib).start()
        v_sib.start()

    @pl.when(s == 1)
    def _():
        k_copy(k_own, 0, 1, sib).wait_recv()
        kown[0] = kbuf[0]
        k_copy(kown, 0, 2, cross).start()
        v_start(EARLY, CHUNKS, 1)

    phi_q = phi_of(halves(proj, turned, low))

    def relay(k, c, slot):
        b = vbuf.at[slot, :, c]
        return remote(b, b, r_send, r_recv.at[k], sib)

    def take(k, c, slot):
        v_copy(k, c, slot).wait_recv()
        relay(k, c, slot).start()

    pl.when(s == 2)(lambda: each(0, HALFWAY, lambda k, c, _: take(k, c, 0)))
    pl.when(s == 3)(lambda: each(0, EARLY, lambda k, c, _: take(k, c, 1)))

    k_two = kbuf.at[pl.ds(0, 2)]

    @pl.when(s == 2)
    def _():
        k_copy(k_two, 0, 2, sib).wait_recv()

    @pl.when(s == 3)
    def _():
        k_copy(k_two, 0, 2, cross).wait_recv()
        k_copy(k_two, 0, 2, sib).start()
        k_copy(k_own, 2, 1, sib).wait_recv()

    @pl.when(s > 0)
    def _():
        keeps, phis, betas, gains = [], [], [], []
        norm = jnp.zeros((1, 128 * NU), F32)
        for r in range(SEGS - 1):
            two = kbuf[r, 0:64, :].astype(F32)
            two_turned = pltpu.roll(two, 64, 1)
            p = jnp.concatenate(
                [halves(two, two_turned, low_half), halves(two_turned, two, low_half)], axis=0
            )
            phi = phi_of(p)
            gates = kbuf[r, 64:80, :].astype(F32)
            beta = gates[0:8] + gates[8:16]
            if r:
                div = jnp.maximum(dot_t(jnp.broadcast_to(norm, (8, 128 * NU)), phi), 1.0)
            keep = jnp.where((idm[0, r + 1] == idm[0, r]) | (s < r + 1), 1.0, 0.0).astype(F32)
            phis.append(phi)
            betas.append(beta[0:1])
            gains.append((beta / div)[0:1] if r else None)
            keeps.append(keep)
            norm = keep * (norm + jnp.sum(phi, axis=0, keepdims=True))
        scale = 1.0 / jnp.maximum(jnp.sum(phi_q * norm, axis=1, keepdims=True), 1.0)
        q = phi_q
        for r in reversed(range(SEGS - 1)):
            q = keeps[r] * q
            t = dot_t(q, phis[r])
            m = t * betas[r] * scale
            mats[:, 128 * r : 128 * (r + 1)] = m.astype(BF16)
            if r:
                q = q - dot(t * gains[r], phis[r])

    def mix_step(c, wide, n):
        v = vbuf[0:n, :, c].reshape(128 * n, wide)
        out[:, c] = jnp.dot(mats[:, : 128 * n], v, preferred_element_type=F32).astype(BF16)

    def mix(c, wide, n):
        if wide <= STEP:
            mix_step(c, wide, n)
        else:

            @pl.loop(0, wide // STEP)
            def _(i):
                mix_step(pl.ds(pl.multiple_of(c.start + i * STEP, 256), STEP), STEP, n)

    @pl.when(s == 0)
    def _():
        out[...] = jnp.zeros_like(out)

    @pl.when(s == 1)
    def _():
        remote(values, vbuf.at[0], d_send, d_recv, sib).wait_recv()
        each(0, CHUNKS, lambda k, c, wide: mix(c, wide, 1))

    def use(k, c, wide, slot, n):
        relay(k, c, 1 - slot).wait_recv()
        mix(c, wide, n)

    @pl.when(s == 2)
    def _():
        each(0, HALFWAY - 1, lambda k, c, wide: use(k, c, wide, 0, 2))

        def body(k, c, wide):
            take(k, c, 0)
            use(k - 1, pl.ds(pl.multiple_of(c.start - wide, 256), wide), wide, 0, 2)

        each(HALFWAY, CHUNKS, body)
        each(CHUNKS - 1, CHUNKS, lambda k, c, wide: use(k, c, wide, 0, 2))
        relay(0, slice(None), 0).wait_send()

    @pl.when(s == 3)
    def _():
        remote(values, vbuf.at[2], d_send, d_recv, sib).wait_recv()

        def body(k, c, wide):
            take(k, c, 1)
            use(k, c, wide, 1, 3)

        each(0, EARLY, lambda k, c, wide: use(k, c, wide, 1, 3))
        each(EARLY, CHUNKS, body)
        relay(0, slice(None), 1).wait_send()

    @pl.when(first)
    def _():
        k_copy(k_own, 0, 1, sib).wait_send()
        v_sib.wait_send()

    @pl.when(second)
    def _():
        for n, sem in ((Z - 1, ring_send), (Z, s_send)):
            b = wbuf.at[pl.ds(0, n)]
            remote(b, b, sem, s_recv.at[0], sib).wait_send()
        b = wbuf.at[0, pl.ds(0, X - 1)]
        remote(b, b, x_send, x_recv, sib).wait_send()
        k_copy(k_two, 0, 2, sib).wait_send()

    @pl.when(s == 3)
    def _():
        remote(pair, pair, y_send, y_recv, sib).wait_send()

    @pl.when(s < 2)
    def _():
        remote(values, vbuf.at[0], v_send, v_recv.at[0], cross).wait_send()


def per_device(hidden, value_states, w_in, w_beta, book_ids):
    _, tokens, width = hidden.shape
    dma = pltpu.SemaphoreType.DMA
    hbm = pl.BlockSpec(memory_space=pltpu.HBM)
    mixed = pl.pallas_call(
        kernel,
        out_shape=jax.ShapeDtypeStruct((tokens, width), BF16),
        in_specs=[hbm] * 5,
        out_specs=pl.BlockSpec(memory_space=pltpu.VMEM),
        scratch_shapes=[
            pltpu.VMEM((tokens, width), BF16),
            pltpu.VMEM((Z, X, YL, 144, 128), BF16),
            pltpu.VMEM((SEGS - 1, tokens, width), BF16),
            pltpu.VMEM((2, 80, 128), BF16),
            pltpu.VMEM((SEGS - 1, 80, 128), BF16),
            pltpu.VMEM((tokens, 128 * (SEGS - 1)), BF16),
            pltpu.VMEM((tokens, 128), F32),
            pltpu.VMEM((tokens, 128), F32),
            pltpu.VMEM((1, 128), BF16), pltpu.SMEM((1, SEGS), jnp.int32),
            pltpu.SemaphoreType.REGULAR, pltpu.SemaphoreType.REGULAR,
            dma, dma, dma, dma, dma, dma, dma, dma, dma, dma((Z // 2, 2)),
            dma, dma((Z // 2 + 1,)), dma, dma((2,)),
            dma, dma((CHUNKS,)), dma, dma((CHUNKS,)), dma, dma,
        ],
        compiler_params=pltpu.CompilerParams(
            collective_id=0, has_side_effects=True, vmem_limit_bytes=32 << 20
        ),
    )(*(
        pltpu.with_memory_space_constraint(a, pltpu.HBM)
        for a in (hidden[0], value_states[0], w_in, w_beta.reshape(1, 128), book_ids)
    ))
    return mixed[None]


def solution(mesh):
    return jax.shard_map(
        per_device,
        mesh=mesh,
        in_specs=(
            P("fsdp", "seg", None),
            P("fsdp", "seg", None),
            P("fsdp", None),
            P("fsdp"),
            P("fsdp", None),
        ),
        out_specs=P("fsdp", "seg", None),
        check_vma=False,
    )
```
